1024 devices in a mesh: row: 16 (over z_hi, y), col: 64 (over z_lo, x, core).
Axes of the slice: x: 4, y: 4, z: 32 (z_hi: 4, z_lo: 8; z = z_hi * 8 + z_lo), core: 2. Of those that a mesh axis runs over, the one named last changes fastest.
Arguments:
- inputs: bfloat16 [512, 8192], P('col', 'row'), may hold values from -6 to 6
- cotangent: bfloat16 [512, 8192], P('col', 'row'), may hold values from -6 to 6
- gate_weight: bfloat16 [8192, 28672], P('row', 'col'), may hold values from -0.09375 to 0.09375
- up_weight: bfloat16 [8192, 28672], P('row', 'col'), may hold values from -0.09375 to 0.09375
- down_weight: bfloat16 [28672, 8192], P('col', 'row'), may hold values from -0.046875 to 0.046875
- gate_pattern: int32 [2048, 28672], P('row', 'col'), may hold values from 0 to 5
- up_pattern: int32 [2048, 28672], P('row', 'col'), may hold values from 0 to 5
- down_pattern: int32 [7168, 8192], P('col', 'row'), may hold values from 0 to 5
Outputs:
- grad_inputs: bfloat16 [512, 8192], P('col', 'row')
- grad_gate_weight: bfloat16 [8192, 28672], P('row', 'col')
- grad_up_weight: bfloat16 [8192, 28672], P('row', 'col')
- grad_down_weight: bfloat16 [28672, 8192], P('col', 'row')
The draws below stay inside these ranges and needn't reach their ends.
Inputs may be any that keep to these rules, and one draw needn't show every extreme that they name: `gate_pattern`: each value names which 2 of its group of 4 weights are kept, as in the reference program. `up_pattern`: each value names which 2 of its group of 4 weights are kept, as in the reference program. `down_pattern`: each value names which 2 of its group of 4 weights are kept, as in the reference program.
All inputs are finite; a program needn't handle non-finite values.
Results may differ from the reference program's by a relative error of at most 0.0049.
Values may be sent and summed in bfloat16 or wider, within the bound.
No kernel may reach another device: no remote copies, remote signals or barrier semaphores. Data moves between devices by JAX's collectives and lax.ppermute only.
A program may use at most 32 MiB of HBM per device.

```python
import functools
import jax
import jax.numpy as jnp

D = 8192
FF = 28672
TOKENS = 512


def set_ends(array, own_key, smallest, largest):
    spot = [jax.random.randint(jax.random.fold_in(own_key, axis), (), 0, length) for axis, length in enumerate(array.shape)]
    longest = array.shape.index(max(array.shape))
    neighbour = spot[:longest] + [(spot[longest] + 1) % array.shape[longest]] + spot[longest + 1:]
    return array.at[tuple(spot)].set(smallest).at[tuple(neighbour)].set(largest)


def level_of(own_key, extent, shards, smallest, high):
    level, own = 1.0, jax.random.fold_in(own_key, 6)
    for dim, shards_of in shards:
        heights = jnp.exp(jax.random.uniform(jax.random.fold_in(own, dim), (shards_of,), jnp.float32, smallest / len(shards), high / len(shards)))
        level = level * jnp.repeat(heights, extent[dim] // shards_of).reshape([-1 if axis == dim else 1 for axis in range(len(extent))])
    return level


def scatter_about(rng, dims, spread, most, shards=(), kind=jnp.bfloat16):
    array = jax.random.normal(rng, dims, jnp.float32) * spread
    if len(shards) > 0:
        array = level_of(rng, dims, shards, -0.22, 0.18) * array
    return jnp.clip(array, min=-most, max=most).astype(kind)


def setup_inputs(seed: int = 0) -> dict:
    arg_keys = jax.random.split(jax.random.key(seed), 9)
    return {
        "inputs": scatter_about(arg_keys[0], (TOKENS, D), 1.0, 6.0, ((0, 64), (1, 16))),
        "cotangent": scatter_about(arg_keys[1], (TOKENS, D), 1.0, 6.0, ((0, 64), (1, 16))),
        "gate_weight": scatter_about(arg_keys[2], (D, FF), (D // 2) ** -0.5, 0.09375, ((0, 16), (1, 64))),
        "up_weight": scatter_about(arg_keys[3], (D, FF), (D // 2) ** -0.5, 0.09375, ((0, 16), (1, 64))),
        "down_weight": scatter_about(arg_keys[4], (FF, D), (FF // 2) ** -0.5, 0.046875, ((0, 64), (1, 16))),
        "gate_pattern": set_ends(jax.random.randint(arg_keys[5], (D // 4, FF), 0, 6), jax.random.fold_in(arg_keys[5], 1), 0, 5).astype(jnp.int32),
        "up_pattern": set_ends(jax.random.randint(arg_keys[6], (D // 4, FF), 0, 6), jax.random.fold_in(arg_keys[6], 1), 0, 5).astype(jnp.int32),
        "down_pattern": set_ends(jax.random.randint(arg_keys[7], (FF // 4, D), 0, 6), jax.random.fold_in(arg_keys[7], 1), 0, 5).astype(jnp.int32),
    }


keep_sets = ((0, 1, 2), (0, 3, 4), (1, 3, 5), (2, 4, 5))


def expand_keep(pattern):
    planes = [functools.reduce(jnp.logical_or, [pattern == member for member in group_set]) for group_set in keep_sets]
    return jnp.stack(planes, axis=1).reshape(pattern.shape[0] * 4, pattern.shape[1])


def sparse(weight, pattern):
    return jnp.where(expand_keep(pattern), weight, jnp.zeros_like(weight))


def swiglu_back(gate_pre, up_pre, hidden_grad):
    sigmoid_gate = jax.nn.sigmoid(gate_pre)
    silu_gate = gate_pre * sigmoid_gate
    hidden = (silu_gate * up_pre).astype(jnp.bfloat16)
    up_grad = (hidden_grad * silu_gate).astype(jnp.bfloat16)
    gate_grad = (hidden_grad * up_pre * sigmoid_gate * (1.0 + gate_pre * (1.0 - sigmoid_gate))).astype(jnp.bfloat16)
    return hidden, gate_grad, up_grad


def reference(inputs, cotangent, gate_weight, up_weight, down_weight, gate_pattern, up_pattern, down_pattern):
    gate_eff = sparse(gate_weight, gate_pattern)
    up_eff = sparse(up_weight, up_pattern)
    down_eff = sparse(down_weight, down_pattern)
    gate_pre = jnp.dot(inputs, gate_eff, preferred_element_type=jnp.float32)
    up_pre = jnp.dot(inputs, up_eff, preferred_element_type=jnp.float32)
    hidden_grad = jnp.dot(cotangent, down_eff.T, preferred_element_type=jnp.float32)
    hidden, gate_grad, up_grad = swiglu_back(gate_pre, up_pre, hidden_grad)
    grad_gate_weight = jnp.where(expand_keep(gate_pattern), jnp.dot(inputs.T, gate_grad, preferred_element_type=jnp.float32), 0.0).astype(jnp.bfloat16)
    grad_up_weight = jnp.where(expand_keep(up_pattern), jnp.dot(inputs.T, up_grad, preferred_element_type=jnp.float32), 0.0).astype(jnp.bfloat16)
    grad_down_weight = jnp.where(expand_keep(down_pattern), jnp.dot(hidden.T, cotangent, preferred_element_type=jnp.float32), 0.0).astype(jnp.bfloat16)
    grad_inputs = (jnp.dot(gate_grad, gate_eff.T, preferred_element_type=jnp.float32) + jnp.dot(up_grad, up_eff.T, preferred_element_type=jnp.float32)).astype(jnp.bfloat16)
    return grad_inputs, grad_gate_weight, grad_up_weight, grad_down_weight
```

```python
import jax
import jax.numpy as jnp
import numpy as np
from jax import lax
from jax.sharding import Mesh, PartitionSpec as P

bf16 = jnp.bfloat16
f32 = jnp.float32
keep_sets = ((0, 1, 2), (0, 3, 4), (1, 3, 5), (2, 4, 5))


def keep_planes(pattern):
    planes = []
    for members in keep_sets:
        kept = pattern == members[0]
        for member in members[1:]:
            kept = kept | (pattern == member)
        planes.append(kept.astype(bf16))
    return planes


def spread_matrix(groups):
    row = lax.broadcasted_iota(jnp.int32, (4 * groups, 4 * groups), 0)
    col = lax.broadcasted_iota(jnp.int32, (4 * groups, 4 * groups), 1)
    return ((row % groups) * 4 + row // groups == col).astype(bf16)


def dot(a, b, dims):
    return lax.dot_general(a, b, (dims, ((), ())), preferred_element_type=f32)


def gather_by_exchange(block, axis, size):
    return lax.all_to_all(jnp.broadcast_to(block[None], (size, *block.shape)), axis, 0, 0)


def swiglu_back(gate_pre, up_pre, hidden_grad):
    sigmoid_gate = jax.nn.sigmoid(gate_pre)
    silu_gate = gate_pre * sigmoid_gate
    hidden = (silu_gate * up_pre).astype(bf16)
    up_grad = (hidden_grad * silu_gate).astype(bf16)
    gate_grad = (
        hidden_grad * up_pre * sigmoid_gate * (1.0 + gate_pre * (1.0 - sigmoid_gate))
    ).astype(bf16)
    return jnp.stack([hidden, gate_grad, up_grad])


def body(inputs, cotangent, gate_weight, up_weight, down_weight, gate_pattern, up_pattern, down_pattern):
    sizes = {"zhi": 4, "y": 4, "zlo": 8, "x": 4, "core": 2}
    rows, width = inputs.shape
    hidden_units = down_weight.shape[0]
    tokens_all = rows * sizes["zlo"] * sizes["x"] * sizes["core"]

    both = jnp.stack([inputs, cotangent])
    both = gather_by_exchange(both, "zlo", sizes["zlo"])
    both = gather_by_exchange(both, "x", sizes["x"])
    both = both.transpose(2, 0, 1, 3, 4).reshape(2, tokens_all // 2, width)
    tokens = lax.all_gather(both[0], "core", axis=0, tiled=True)
    grad_out = lax.all_gather(both[1], "core", axis=0, tiled=True)

    spread_width = spread_matrix(width // 4)
    spread_units = spread_matrix(hidden_units // 4)
    gate_keep = dot(jnp.concatenate(keep_planes(gate_pattern.T), axis=1), spread_width, ((1,), (0,))) > 0.5
    up_keep = dot(jnp.concatenate(keep_planes(up_pattern.T), axis=1), spread_width, ((1,), (0,))) > 0.5
    down_keep = dot(spread_units, jnp.concatenate(keep_planes(down_pattern), axis=0), ((0,), (0,))) > 0.5
    zero = jnp.zeros((), bf16)
    gate_eff = jnp.where(gate_keep, gate_weight.T, zero)
    up_eff = jnp.where(up_keep, up_weight.T, zero)
    down_eff = jnp.where(down_keep, down_weight, zero)

    ny, nz = sizes["y"], sizes["zhi"]
    quarter, strip = hidden_units // ny, tokens_all // nz
    partial = jnp.stack(
        [
            dot(gate_eff, tokens, ((1,), (1,))).reshape(ny, quarter, tokens_all),
            dot(up_eff, tokens, ((1,), (1,))).reshape(ny, quarter, tokens_all),
            dot(down_eff, grad_out, ((1,), (1,))).reshape(ny, quarter, tokens_all),
        ],
        axis=1,
    )
    summed = lax.all_to_all(partial, "y", 0, 0).sum(axis=0)
    strips = summed.astype(bf16).reshape(3, quarter, nz, strip).transpose(2, 0, 1, 3)
    summed = lax.all_to_all(strips, "zhi", 0, 0).astype(f32).sum(axis=0)
    triple = swiglu_back(summed[0], summed[1], summed[2])
    triple = gather_by_exchange(triple, "zhi", nz)
    triple = gather_by_exchange(triple, "y", ny)
    triple = triple.transpose(2, 0, 3, 1, 4).reshape(3, hidden_units, tokens_all)
    hidden, gate_grad, up_grad = triple[0], triple[1], triple[2]

    half = tokens_all // 2
    back = dot(gate_grad, gate_eff, ((0,), (0,))) + dot(up_grad, up_eff, ((0,), (0,)))
    back = back.reshape(2, half, width)
    core = lax.axis_index("core")
    kept = jnp.where(core == 0, back[0], back[1])
    sent = jnp.where(core == 0, back[1], back[0])
    back = kept + lax.ppermute(sent, "core", [(0, 1), (1, 0)])
    back = lax.all_to_all(back.reshape(sizes["x"], half // sizes["x"], width), "x", 0, 0).sum(axis=0)
    back = lax.all_to_all(back.reshape(sizes["zlo"], rows, width), "zlo", 0, 0).sum(axis=0)

    grad_gate = jnp.where(gate_keep, dot(gate_grad, tokens, ((1,), (0,))), 0.0).astype(bf16)
    grad_up = jnp.where(up_keep, dot(up_grad, tokens, ((1,), (0,))), 0.0).astype(bf16)
    grad_down = jnp.where(down_keep, dot(hidden, grad_out, ((1,), (0,))), 0.0).astype(bf16)
    return (back.astype(bf16), grad_gate.T, grad_up.T, grad_down)


def solution(mesh):
    fine = Mesh(
        np.asarray(mesh.devices).reshape(4, 4, 8, 4, 2), ("zhi", "y", "zlo", "x", "core")
    )
    row, col = ("zhi", "y"), ("zlo", "x", "core")
    return jax.shard_map(
        body,
        mesh=fine,
        in_specs=(
            P(col, row),
            P(col, row),
            P(row, col),
            P(row, col),
            P(col, row),
            P(row, col),
            P(row, col),
            P(col, row),
        ),
        out_specs=(P(col, row), P(row, col), P(row, col), P(col, row)),
        check_vma=False,
    )
```

```python
import jax
import jax.numpy as jnp
import numpy as np
from jax import lax
from jax.sharding import Mesh, PartitionSpec as P

bf16 = jnp.bfloat16
f32 = jnp.float32
keep_sets = ((0, 1, 2), (0, 3, 4), (1, 3, 5), (2, 4, 5))


def keep_planes(pattern):
    planes = []
    for members in keep_sets:
        kept = pattern == members[0]
        for member in members[1:]:
            kept = kept | (pattern == member)
        planes.append(kept.astype(bf16))
    return planes


def spread_matrix(groups):
    row = lax.broadcasted_iota(jnp.int32, (4 * groups, 4 * groups), 0)
    col = lax.broadcasted_iota(jnp.int32, (4 * groups, 4 * groups), 1)
    return ((row % groups) * 4 + row // groups == col).astype(bf16)


def dot(a, b, dims):
    return lax.dot_general(a, b, (dims, ((), ())), preferred_element_type=f32)


def gather_by_exchange(block, axis, size):
    return lax.all_to_all(jnp.broadcast_to(block[None], (size, *block.shape)), axis, 0, 0)


def zhi_exchange(block, flip0, flip1):
    pairs = [
        (z * 2 + c, (z ^ (flip0, flip1)[c]) * 2 + c) for z in range(4) for c in range(2)
    ]
    return lax.ppermute(block, ("zhi", "core"), pairs)


def swiglu_back(gate_pre, up_pre, hidden_grad):
    sigmoid_gate = jax.nn.sigmoid(gate_pre)
    silu_gate = gate_pre * sigmoid_gate
    hidden = (silu_gate * up_pre).astype(bf16)
    up_grad = (hidden_grad * silu_gate).astype(bf16)
    gate_grad = (
        hidden_grad * up_pre * sigmoid_gate * (1.0 + gate_pre * (1.0 - sigmoid_gate))
    ).astype(bf16)
    return jnp.stack([hidden, gate_grad, up_grad])


def body(inputs, cotangent, gate_weight, up_weight, down_weight, gate_pattern, up_pattern, down_pattern):
    sizes = {"zhi": 4, "y": 4, "zlo": 8, "x": 4, "core": 2}
    rows, width = inputs.shape
    hidden_units = down_weight.shape[0]
    tokens_all = rows * sizes["zlo"] * sizes["x"] * sizes["core"]

    both = jnp.stack([inputs, cotangent])
    both = gather_by_exchange(both, "zlo", sizes["zlo"])
    both = gather_by_exchange(both, "x", sizes["x"])
    both = both.transpose(2, 0, 1, 3, 4).reshape(2, tokens_all // 2, width)
    tokens = lax.all_gather(both[0], "core", axis=0, tiled=True)
    grad_out = lax.all_gather(both[1], "core", axis=0, tiled=True)

    spread_width = spread_matrix(width // 4)
    spread_units = spread_matrix(hidden_units // 4)
    gate_keep = dot(jnp.concatenate(keep_planes(gate_pattern.T), axis=1), spread_width, ((1,), (0,))) > 0.5
    up_keep = dot(jnp.concatenate(keep_planes(up_pattern.T), axis=1), spread_width, ((1,), (0,))) > 0.5
    down_keep = dot(spread_units, jnp.concatenate(keep_planes(down_pattern), axis=0), ((0,), (0,))) > 0.5
    zero = jnp.zeros((), bf16)
    gate_eff = jnp.where(gate_keep, gate_weight.T, zero)
    up_eff = jnp.where(up_keep, up_weight.T, zero)
    down_eff = jnp.where(down_keep, down_weight, zero)

    ny = sizes["y"]
    quarter = hidden_units // ny
    partial = jnp.stack(
        [
            dot(gate_eff, tokens, ((1,), (1,))).reshape(ny, quarter, tokens_all),
            dot(up_eff, tokens, ((1,), (1,))).reshape(ny, quarter, tokens_all),
            dot(down_eff, grad_out, ((1,), (1,))).reshape(ny, quarter, tokens_all),
        ],
        axis=1,
    )
    summed = lax.all_to_all(partial, "y", 0, 0).sum(axis=0)

    zhi, core = lax.axis_index("zhi"), lax.axis_index("core")
    first = jnp.where(core == 0, (zhi ^ (zhi >> 1)) & 1, zhi >> 1) == 0
    front, back = summed[:, :, : tokens_all // 2], summed[:, :, tokens_all // 2 :]
    kept = jnp.where(first, front, back)
    sent = jnp.where(first, back, front).astype(bf16)
    kept = kept + zhi_exchange(sent, 1, 3).astype(f32)
    kept = kept + zhi_exchange(kept.astype(bf16), 3, 1).astype(f32)
    mine = swiglu_back(kept[0], kept[1], kept[2])
    other = zhi_exchange(mine, 1, 3)
    triple = jnp.concatenate(
        [jnp.where(first, mine, other), jnp.where(first, other, mine)], axis=2
    )
    triple = gather_by_exchange(triple, "y", ny)
    triple = triple.transpose(1, 0, 2, 3).reshape(3, hidden_units, tokens_all)
    hidden, gate_grad, up_grad = triple[0], triple[1], triple[2]

    half = tokens_all // 2
    back = dot(gate_grad, gate_eff, ((0,), (0,))) + dot(up_grad, up_eff, ((0,), (0,)))
    back = back.reshape(2, half, width)
    kept = jnp.where(core == 0, back[0], back[1])
    sent = jnp.where(core == 0, back[1], back[0])
    back = kept + lax.ppermute(sent, "core", [(0, 1), (1, 0)])
    back = lax.all_to_all(back.reshape(sizes["x"], half // sizes["x"], width), "x", 0, 0).sum(axis=0)
    back = lax.all_to_all(back.reshape(sizes["zlo"], rows, width), "zlo", 0, 0).sum(axis=0)

    grad_gate = jnp.where(gate_keep, dot(gate_grad, tokens, ((1,), (0,))), 0.0).astype(bf16)
    grad_up = jnp.where(up_keep, dot(up_grad, tokens, ((1,), (0,))), 0.0).astype(bf16)
    grad_down = jnp.where(down_keep, dot(hidden, grad_out, ((1,), (0,))), 0.0).astype(bf16)
    return (back.astype(bf16), grad_gate.T, grad_up.T, grad_down)


def solution(mesh):
    fine = Mesh(
        np.asarray(mesh.devices).reshape(4, 4, 8, 4, 2), ("zhi", "y", "zlo", "x", "core")
    )
    row, col = ("zhi", "y"), ("zlo", "x", "core")
    return jax.shard_map(
        body,
        mesh=fine,
        in_specs=(
            P(col, row),
            P(col, row),
            P(row, col),
            P(row, col),
            P(col, row),
            P(row, col),
            P(row, col),
            P(col, row),
        ),
        out_specs=(P(col, row), P(row, col), P(row, col), P(col, row)),
        check_vma=False,
    )
```

```python
import jax
import jax.numpy as jnp
import numpy as np
from jax import lax
from jax.sharding import Mesh, PartitionSpec as P

bf16 = jnp.bfloat16
f32 = jnp.float32
keep_sets = ((0, 1, 2), (0, 3, 4), (1, 3, 5), (2, 4, 5))


def keep_planes(pattern):
    planes = []
    for members in keep_sets:
        kept = pattern == members[0]
        for member in members[1:]:
            kept = kept | (pattern == member)
        planes.append(kept.astype(bf16))
    return planes


def spread_matrix(groups):
    row = lax.broadcasted_iota(jnp.int32, (4 * groups, 4 * groups), 0)
    col = lax.broadcasted_iota(jnp.int32, (4 * groups, 4 * groups), 1)
    return ((row % groups) * 4 + row // groups == col).astype(bf16)


def dot(a, b, dims):
    return lax.dot_general(a, b, (dims, ((), ())), preferred_element_type=f32)


def gather_by_exchange(block, axis, size):
    return lax.all_to_all(jnp.broadcast_to(block[None], (size, *block.shape)), axis, 0, 0)


def zhi_exchange(block, flip0, flip1):
    pairs = [
        (z * 2 + c, (z ^ (flip0, flip1)[c]) * 2 + c) for z in range(4) for c in range(2)
    ]
    return lax.ppermute(block, ("zhi", "core"), pairs)


f16 = jnp.float16
PAD = 8


def to_link(values, power):
    scaled = values * jnp.exp2(-power)
    shape = (*values.shape[:-2], PAD, values.shape[-1])
    return jnp.concatenate([scaled, jnp.broadcast_to(power, shape)], axis=-2).astype(f16)


def from_link(block):
    wide = block.astype(f32)
    power = wide[..., -PAD : 1 - PAD, :1]
    return wide[..., :-PAD, :] * jnp.exp2(power), power


def top(values):
    return jnp.max(jnp.abs(values)).astype(f32)


def power_of(bound):
    return jnp.ceil(jnp.log2(jnp.maximum(bound, 1e-30))) - 15.0


def swiglu_back(gate_pre, up_pre, hidden_grad):
    sigmoid_gate = jax.nn.sigmoid(gate_pre)
    silu_gate = gate_pre * sigmoid_gate
    hidden = (silu_gate * up_pre).astype(bf16)
    up_grad = (hidden_grad * silu_gate).astype(bf16)
    gate_grad = (
        hidden_grad * up_pre * sigmoid_gate * (1.0 + gate_pre * (1.0 - sigmoid_gate))
    ).astype(bf16)
    return jnp.stack([hidden, gate_grad, up_grad])


def body(inputs, cotangent, gate_weight, up_weight, down_weight, gate_pattern, up_pattern, down_pattern):
    sizes = {"zhi": 4, "y": 4, "zlo": 8, "x": 4, "core": 2}
    rows, width = inputs.shape
    hidden_units = down_weight.shape[0]
    half = rows * sizes["zlo"] * sizes["x"]
    ny = sizes["y"]
    quarter = hidden_units // ny
    zhi, core = lax.axis_index("zhi"), lax.axis_index("core")

    keep = jnp.where(core == 0, (zhi ^ (zhi >> 1)) & 1, zhi >> 1)
    own_first = keep == core

    spread_width = spread_matrix(width // 4)
    spread_units = spread_matrix(hidden_units // 4)
    gate_keep = dot(jnp.concatenate(keep_planes(gate_pattern.T), axis=1), spread_width, ((1,), (0,))) > 0.5
    up_keep = dot(jnp.concatenate(keep_planes(up_pattern.T), axis=1), spread_width, ((1,), (0,))) > 0.5
    down_keep = dot(spread_units, jnp.concatenate(keep_planes(down_pattern), axis=0), ((0,), (0,))) > 0.5
    zero = jnp.zeros((), bf16)
    gate_eff = jnp.where(gate_keep, gate_weight.T, zero)
    up_eff = jnp.where(up_keep, up_weight.T, zero)
    down_eff = jnp.where(down_keep, down_weight, zero)
    weight_tops = jnp.stack([top(gate_weight), top(up_weight), top(down_weight)])

    both = jnp.stack([inputs, cotangent])
    both = gather_by_exchange(both, "zlo", sizes["zlo"])
    both = gather_by_exchange(both, "x", sizes["x"])
    own = both.transpose(2, 0, 1, 3, 4).reshape(2, half, width)
    other = lax.ppermute(own, "core", [(0, 1), (1, 0)])
    kept_side = jnp.where(own_first, own, other)
    sent_side = jnp.where(own_first, other, own)
    token_tops = jnp.maximum(
        jnp.max(jnp.abs(own), axis=(1, 2)), jnp.max(jnp.abs(other), axis=(1, 2))
    ).astype(f32)
    bounds = weight_tops * jnp.stack([token_tops[0], token_tops[0], token_tops[1]])
    power = power_of(bounds * (width / 2))[:, None, None]

    def summed_over_y(side):
        partial = jnp.stack(
            [
                dot(gate_eff, side[0], ((1,), (1,))).reshape(ny, quarter, half),
                dot(up_eff, side[0], ((1,), (1,))).reshape(ny, quarter, half),
                dot(down_eff, side[1], ((1,), (1,))).reshape(ny, quarter, half),
            ],
            axis=1,
        )
        values, powers = from_link(lax.all_to_all(to_link(partial, power), "y", 0, 0))
        return values.sum(axis=0), powers.max(axis=0) + 2.0

    sent, sent_power = summed_over_y(sent_side)
    values, _ = from_link(zhi_exchange(to_link(sent, sent_power), 1, 3))
    kept, kept_power = summed_over_y(kept_side)
    kept = kept + values
    values, _ = from_link(zhi_exchange(to_link(kept, kept_power + 4.0), 3, 1))
    kept = kept + values

    mine = swiglu_back(kept[0], kept[1], kept[2])
    theirs = zhi_exchange(mine, 1, 3)

    def units(block):
        block = gather_by_exchange(block, "y", ny)
        return block.transpose(1, 0, 2, 3).reshape(3, hidden_units, half)

    first, second = units(mine), units(theirs)

    def back_of(side):
        return dot(side[1], gate_eff, ((0,), (0,))) + dot(side[2], up_eff, ((0,), (0,)))

    back_first, back_second = back_of(first), back_of(second)
    stays = jnp.where(own_first, back_first, back_second)
    leaves = jnp.where(own_first, back_second, back_first)
    back = stays + lax.ppermute(leaves, "core", [(0, 1), (1, 0)])
    back = lax.all_to_all(back.reshape(sizes["x"], half // sizes["x"], width), "x", 0, 0).sum(axis=0)
    back = lax.all_to_all(back.reshape(sizes["zlo"], rows, width), "zlo", 0, 0).sum(axis=0)

    def weight_grad(member, side):
        return dot(first[member], kept_side[side], ((1,), (0,))) + dot(
            second[member], sent_side[side], ((1,), (0,))
        )

    grad_gate = jnp.where(gate_keep, weight_grad(1, 0), 0.0).astype(bf16)
    grad_up = jnp.where(up_keep, weight_grad(2, 0), 0.0).astype(bf16)
    grad_down = jnp.where(down_keep, weight_grad(0, 1), 0.0).astype(bf16)
    return (back.astype(bf16), grad_gate.T, grad_up.T, grad_down)


def solution(mesh):
    fine = Mesh(
        np.asarray(mesh.devices).reshape(4, 4, 8, 4, 2), ("zhi", "y", "zlo", "x", "core")
    )
    row, col = ("zhi", "y"), ("zlo", "x", "core")
    return jax.shard_map(
        body,
        mesh=fine,
        in_specs=(
            P(col, row),
            P(col, row),
            P(row, col),
            P(row, col),
            P(col, row),
            P(row, col),
            P(row, col),
            P(col, row),
        ),
        out_specs=(P(col, row), P(row, col), P(row, col), P(col, row)),
        check_vma=False,
    )
```

```python
import jax
import jax.numpy as jnp
import numpy as np
from jax import lax
from jax.experimental import pallas as pl
from jax.experimental.pallas import tpu as pltpu
from jax.sharding import Mesh, PartitionSpec as P

bf16 = jnp.bfloat16
f32 = jnp.float32
keep_sets = ((0, 1, 2), (0, 3, 4), (1, 3, 5), (2, 4, 5))


def keep_planes(pattern):
    planes = []
    for members in keep_sets:
        kept = pattern == members[0]
        for member in members[1:]:
            kept = kept | (pattern == member)
        planes.append(kept.astype(bf16))
    return planes


def spread_matrix(groups):
    row = lax.broadcasted_iota(jnp.int32, (4 * groups, 4 * groups), 0)
    col = lax.broadcasted_iota(jnp.int32, (4 * groups, 4 * groups), 1)
    return ((row % groups) * 4 + row // groups == col).astype(bf16)


def dot(a, b, dims):
    return lax.dot_general(a, b, (dims, ((), ())), preferred_element_type=f32)


def gather_by_exchange(block, axis, size):
    return lax.all_to_all(jnp.broadcast_to(block[None], (size, *block.shape)), axis, 0, 0)


def zhi_exchange(block, flip0, flip1):
    pairs = [
        (z * 2 + c, (z ^ (flip0, flip1)[c]) * 2 + c) for z in range(4) for c in range(2)
    ]
    return lax.ppermute(block, ("zhi", "core"), pairs)


EXTRA = 16


def pack(values):
    rows, powers = [], []
    for value in values:
        most = jnp.max(jnp.abs(value), axis=0, keepdims=True)
        power = jnp.ceil(jnp.log2(jnp.maximum(most, 1e-30))) - 14.0
        rows.append(to_int16(jnp.round(value * jnp.exp2(-power))))
        powers.append(power)
    spot = lax.broadcasted_iota(jnp.int32, (EXTRA, values[0].shape[1]), 0)
    tail = jnp.where(spot == 0, powers[0], jnp.where(spot == 1, powers[1], powers[2]))
    return rows, to_int16(tail)


def to_int16(values):
    return values.astype(jnp.int32).astype(jnp.int16)


def wide(block):
    return block.astype(jnp.int32).astype(f32)


def unpack(block, units):
    powers = wide(block[3 * units : 3 * units + EXTRA, :])
    return [
        wide(block[i * units : (i + 1) * units, :]) * jnp.exp2(powers[i : i + 1, :])
        for i in range(3)
    ]


def partial_kernel(gate_ref, up_ref, down_ref, own_ref, other_ref, out_ref):
    ny, units = out_ref.shape[0], gate_ref.shape[0] // out_ref.shape[0]
    half = own_ref.shape[1]
    for spot, side in enumerate((own_ref, other_ref)):
        products = [
            dot(gate_ref[...], side[0], ((1,), (1,))),
            dot(up_ref[...], side[0], ((1,), (1,))),
            dot(down_ref[...], side[1], ((1,), (1,))),
        ]
        for c in range(ny):
            rows, tail = pack([p[c * units : (c + 1) * units] for p in products])
            for i in range(3):
                out_ref[c, i * units : (i + 1) * units, spot * half : (spot + 1) * half] = rows[i]
            out_ref[c, 3 * units :, spot * half : (spot + 1) * half] = tail


def first_sum_kernel(block_ref, *outs):
    ny, units = block_ref.shape[0], outs[0].shape[1]
    half = outs[0].shape[2]
    for spot in range(2):
        lanes = slice(spot * half, (spot + 1) * half)
        total = [0.0, 0.0, 0.0]
        for c in range(ny):
            powers = wide(block_ref[c, 3 * units :, lanes])
            for i in range(3):
                total[i] += wide(block_ref[c, i * units : (i + 1) * units, lanes]) * jnp.exp2(
                    powers[i : i + 1, :]
                )
        store(total, outs[2 * spot], outs[2 * spot + 1])


def store(total, total_ref, send_ref):
    units = total_ref.shape[1]
    rows, tail = pack(total)
    for i in range(3):
        total_ref[i] = total[i]
        send_ref[i * units : (i + 1) * units, :] = rows[i]
    send_ref[3 * units :, :] = tail


def next_sum_kernel(total_ref, block_ref, out_ref, send_ref):
    parts = unpack(block_ref, total_ref.shape[1])
    store([total_ref[i] + parts[i] for i in range(3)], out_ref, send_ref)


def swiglu_kernel(total_ref, block_ref, out_ref):
    units = total_ref.shape[1]
    parts = unpack(block_ref, units)
    gate_pre, up_pre, hidden_grad = [total_ref[i] + parts[i] for i in range(3)]
    sigmoid_gate = jax.nn.sigmoid(gate_pre)
    silu_gate = gate_pre * sigmoid_gate
    results = (
        silu_gate * up_pre,
        hidden_grad * up_pre * sigmoid_gate * (1.0 + gate_pre * (1.0 - sigmoid_gate)),
        hidden_grad * silu_gate,
    )
    for i, result in enumerate(results):
        result = result.astype(bf16)
        for c in range(out_ref.shape[0]):
            out_ref[c, i * units : (i + 1) * units, :] = result


def call(kernel, outs, *args):
    return pl.pallas_call(
        kernel,
        out_shape=[jax.ShapeDtypeStruct(shape, kind) for shape, kind in outs],
        compiler_params=pltpu.CompilerParams(vmem_limit_bytes=32 * 2**20),
        cost_estimate=pl.CostEstimate(flops=2 * 10**10, bytes_accessed=1024, transcendentals=0),
    )(*args)


def body(inputs, cotangent, gate_weight, up_weight, down_weight, gate_pattern, up_pattern, down_pattern):
    sizes = {"zhi": 4, "y": 4, "zlo": 8, "x": 4, "core": 2}
    rows, width = inputs.shape
    hidden_units = down_weight.shape[0]
    half = rows * sizes["zlo"] * sizes["x"]
    ny = sizes["y"]
    quarter = hidden_units // ny
    spread_width = spread_matrix(width // 4)
    spread_units = spread_matrix(hidden_units // 4)
    gate_keep = dot(jnp.concatenate(keep_planes(gate_pattern.T), axis=1), spread_width, ((1,), (0,))) > 0.5
    up_keep = dot(jnp.concatenate(keep_planes(up_pattern.T), axis=1), spread_width, ((1,), (0,))) > 0.5
    down_keep = dot(spread_units, jnp.concatenate(keep_planes(down_pattern), axis=0), ((0,), (0,))) > 0.5
    zero = jnp.zeros((), bf16)
    gate_eff = jnp.where(gate_keep, gate_weight.T, zero)
    up_eff = jnp.where(up_keep, up_weight.T, zero)
    down_eff = jnp.where(down_keep, down_weight, zero)

    swap = [(0, 1), (1, 0)]
    both = jnp.stack([inputs, cotangent])
    both = gather_by_exchange(both, "zlo", sizes["zlo"])
    both = gather_by_exchange(both, "x", sizes["x"])
    own = both.transpose(2, 0, 1, 3, 4).reshape(2, half, width)
    other = lax.ppermute(own, "core", swap)

    i16 = jnp.int16
    packed = 3 * quarter + EXTRA
    (block,) = call(
        partial_kernel,
        [((ny, packed, 2 * half), i16)],
        gate_eff, up_eff, down_eff, own, other,
    )
    block = lax.all_to_all(block, "y", 0, 0)

    pair = [((3, quarter, half), f32), ((packed, half), i16)]
    total1, send1, total2, send2 = call(first_sum_kernel, pair + pair, block)
    got1 = zhi_exchange(send1, 1, 3)
    got2 = zhi_exchange(send2, 1, 3)
    total1, send1 = call(next_sum_kernel, pair, total1, got1)
    got1 = zhi_exchange(send1, 3, 1)
    total2, send2 = call(next_sum_kernel, pair, total2, got2)
    got2 = zhi_exchange(send2, 3, 1)
    spread = [((ny, 3 * quarter, half), bf16)]
    (spread1,) = call(swiglu_kernel, spread, total1, got1)
    second = lax.all_to_all(spread1, "y", 0, 0)
    (spread2,) = call(swiglu_kernel, spread, total2, got2)
    first = lax.all_to_all(spread2, "y", 0, 0)

    def units(block):
        block = block.reshape(ny, 3, quarter, half)
        return block.transpose(1, 0, 2, 3).reshape(3, hidden_units, half)

    first, second = units(first), units(second)

    def back_of(side):
        return dot(side[1], gate_eff, ((0,), (0,))) + dot(side[2], up_eff, ((0,), (0,)))

    back = back_of(second) + lax.ppermute(back_of(first), "core", swap)
    back = lax.all_to_all(back.reshape(sizes["x"], half // sizes["x"], width), "x", 0, 0).sum(axis=0)
    back = lax.all_to_all(back.reshape(sizes["zlo"], rows, width), "zlo", 0, 0).sum(axis=0)

    def weight_grad(member, side):
        return dot(first[member], other[side], ((1,), (0,))) + dot(
            second[member], own[side], ((1,), (0,))
        )

    grad_gate = jnp.where(gate_keep, weight_grad(1, 0), 0.0).astype(bf16)
    grad_up = jnp.where(up_keep, weight_grad(2, 0), 0.0).astype(bf16)
    grad_down = jnp.where(down_keep, weight_grad(0, 1), 0.0).astype(bf16)
    return (back.astype(bf16), grad_gate.T, grad_up.T, grad_down)


def solution(mesh):
    fine = Mesh(
        np.asarray(mesh.devices).reshape(4, 4, 8, 4, 2), ("zhi", "y", "zlo", "x", "core")
    )
    row, col = ("zhi", "y"), ("zlo", "x", "core")
    return jax.shard_map(
        body,
        mesh=fine,
        in_specs=(
            P(col, row),
            P(col, row),
            P(row, col),
            P(row, col),
            P(col, row),
            P(row, col),
            P(row, col),
            P(col, row),
        ),
        out_specs=(P(col, row), P(row, col), P(row, col), P(col, row)),
        check_vma=False,
    )
```

```python
import jax
import jax.numpy as jnp
import numpy as np
from jax import lax
from jax.experimental import pallas as pl
from jax.experimental.pallas import tpu as pltpu
from jax.sharding import Mesh, PartitionSpec as P

bf16 = jnp.bfloat16
f32 = jnp.float32
keep_sets = ((0, 1, 2), (0, 3, 4), (1, 3, 5), (2, 4, 5))


def keep_planes(pattern):
    planes = []
    for members in keep_sets:
        kept = pattern == members[0]
        for member in members[1:]:
            kept = kept | (pattern == member)
        planes.append(kept.astype(bf16))
    return planes


def spread_matrix(groups):
    row = lax.broadcasted_iota(jnp.int32, (4 * groups, 4 * groups), 0)
    col = lax.broadcasted_iota(jnp.int32, (4 * groups, 4 * groups), 1)
    return ((row % groups) * 4 + row // groups == col).astype(bf16)


def dot(a, b, dims):
    return lax.dot_general(a, b, (dims, ((), ())), preferred_element_type=f32)


def zhi_exchange(block, flip0, flip1):
    pairs = [
        (z * 2 + c, (z ^ (flip0, flip1)[c]) * 2 + c) for z in range(4) for c in range(2)
    ]
    return lax.ppermute(block, ("zhi", "core"), pairs)


EXTRA = 16
COST = 2 * 10**9


def pack(values):
    rows, powers = [], []
    for value in values:
        most = jnp.max(jnp.abs(value), axis=0, keepdims=True)
        power = jnp.ceil(jnp.log2(jnp.maximum(most, 1e-30))) - 14.0
        rows.append(to_int16(jnp.round(value * jnp.exp2(-power))))
        powers.append(power)
    spot = lax.broadcasted_iota(jnp.int32, (EXTRA, values[0].shape[1]), 0)
    tail = jnp.where(spot == 0, powers[0], jnp.where(spot == 1, powers[1], powers[2]))
    return rows, to_int16(tail)


def to_int16(values):
    return values.astype(jnp.int32).astype(jnp.int16)


def wide(block):
    return block.astype(jnp.int32).astype(f32)


def unpack(block, units):
    powers = wide(block[3 * units : 3 * units + EXTRA, :])
    return [
        wide(block[i * units : (i + 1) * units, :]) * jnp.exp2(powers[i : i + 1, :])
        for i in range(3)
    ]


def spread_kernel(*refs):
    out_ref = refs[-1]
    for c in range(out_ref.shape[0]):
        if len(refs) == 2:
            out_ref[c] = refs[0][...]
        else:
            for i, ref in enumerate(refs[:-1]):
                out_ref[c, i] = ref[...]


def partial_kernel(flag_ref, gate_ref, up_ref, down_ref, own_ref, other_ref, out_ref):
    ny, units = out_ref.shape[0], gate_ref.shape[0] // out_ref.shape[0]
    is_own = flag_ref[0] == 1
    tokens = jnp.where(is_own, own_ref[0], other_ref[0])
    grad_out = jnp.where(is_own, own_ref[1], other_ref[1])
    products = [
        dot(gate_ref[...], tokens, ((1,), (1,))),
        dot(up_ref[...], tokens, ((1,), (1,))),
        dot(down_ref[...], grad_out, ((1,), (1,))),
    ]
    for c in range(ny):
        store([p[c * units : (c + 1) * units] for p in products], out_ref.at[c])


def store(values, send_ref):
    units = values[0].shape[0]
    rows, tail = pack(values)
    for i in range(3):
        send_ref[i * units : (i + 1) * units, :] = rows[i]
    send_ref[3 * units :, :] = tail


def sum_over_blocks(block_ref):
    units = (block_ref.shape[1] - EXTRA) // 3
    total = [0.0, 0.0, 0.0]
    for c in range(block_ref.shape[0]):
        parts = unpack(block_ref.at[c], units)
        total = [total[i] + parts[i] for i in range(3)]
    return total


def sent_sum_kernel(block_ref, send_ref):
    store(sum_over_blocks(block_ref), send_ref)


def kept_sum_kernel(block_ref, got_ref, total_ref, send_ref):
    total = sum_over_blocks(block_ref)
    parts = unpack(got_ref, total_ref.shape[1])
    total = [total[i] + parts[i] for i in range(3)]
    for i in range(3):
        total_ref[i] = total[i]
    store(total, send_ref)


def swiglu_kernel(total_ref, got_ref, out_ref, spread_ref):
    units = total_ref.shape[1]
    parts = unpack(got_ref, units)
    gate_pre, up_pre, hidden_grad = [total_ref[i] + parts[i] for i in range(3)]
    sigmoid_gate = jax.nn.sigmoid(gate_pre)
    silu_gate = gate_pre * sigmoid_gate
    results = (
        silu_gate * up_pre,
        hidden_grad * up_pre * sigmoid_gate * (1.0 + gate_pre * (1.0 - sigmoid_gate)),
        hidden_grad * silu_gate,
    )
    for i, result in enumerate(results):
        result = result.astype(bf16)
        out_ref[i * units : (i + 1) * units, :] = result
        for c in range(spread_ref.shape[0]):
            spread_ref[c, i * units : (i + 1) * units, :] = result


def call(kernel, outs, *args, scalars=0):
    places = [pltpu.SMEM] * scalars + [pltpu.VMEM] * (len(args) - scalars)
    return pl.pallas_call(
        kernel,
        in_specs=[pl.BlockSpec(memory_space=place) for place in places],
        out_shape=[jax.ShapeDtypeStruct(shape, kind) for shape, kind in outs],
        compiler_params=pltpu.CompilerParams(vmem_limit_bytes=32 * 2**20),
        cost_estimate=pl.CostEstimate(flops=COST, bytes_accessed=1024, transcendentals=0),
    )(*args)


def body(inputs, cotangent, gate_weight, up_weight, down_weight, gate_pattern, up_pattern, down_pattern):
    sizes = {"zhi": 4, "y": 4, "zlo": 8, "x": 4, "core": 2}
    rows, width = inputs.shape
    hidden_units = down_weight.shape[0]
    half = rows * sizes["zlo"] * sizes["x"]
    ny = sizes["y"]
    quarter = hidden_units // ny
    spread_width = spread_matrix(width // 4)
    spread_units = spread_matrix(hidden_units // 4)
    gate_keep = dot(jnp.concatenate(keep_planes(gate_pattern.T), axis=1), spread_width, ((1,), (0,))) > 0.5
    up_keep = dot(jnp.concatenate(keep_planes(up_pattern.T), axis=1), spread_width, ((1,), (0,))) > 0.5
    down_keep = dot(spread_units, jnp.concatenate(keep_planes(down_pattern), axis=0), ((0,), (0,))) > 0.5
    zero = jnp.zeros((), bf16)
    gate_eff = jnp.where(gate_keep, gate_weight.T, zero)
    up_eff = jnp.where(up_keep, up_weight.T, zero)
    down_eff = jnp.where(down_keep, down_weight, zero)

    swap = [(0, 1), (1, 0)]
    nx, nzlo = sizes["x"], sizes["zlo"]
    (both,) = call(spread_kernel, [((nzlo, 2, rows, width), bf16)], inputs, cotangent)
    both = lax.all_to_all(both, "zlo", 0, 0)
    both, gate_eff, up_eff, down_eff = lax.optimization_barrier(
        (both, gate_eff, up_eff, down_eff)
    )
    (both,) = call(spread_kernel, [((nx, nzlo, 2, rows, width), bf16)], both)
    both = lax.all_to_all(both, "x", 0, 0)
    own = both.transpose(2, 0, 1, 3, 4).reshape(2, half, width)
    other = lax.ppermute(own, "core", swap)

    zhi, core = lax.axis_index("zhi"), lax.axis_index("core")
    keep = jnp.where(core == 0, (zhi ^ (zhi >> 1)) & 1, zhi >> 1)
    own_kept = keep == core
    flag = own_kept.astype(jnp.int32).reshape(1)

    i16 = jnp.int16
    packed = 3 * quarter + EXTRA
    block = [((ny, packed, half), i16)]
    operands = (gate_eff, up_eff, down_eff, own, other)
    (sent,) = call(partial_kernel, block, 1 - flag, *operands, scalars=1)
    (kept,) = call(partial_kernel, block, flag, *operands, scalars=1)
    sent = lax.all_to_all(sent, "y", 0, 0)
    (send,) = call(sent_sum_kernel, [((packed, half), i16)], sent)
    got = zhi_exchange(send, 1, 3)
    kept = lax.all_to_all(kept, "y", 0, 0)
    total, send = call(
        kept_sum_kernel, [((3, quarter, half), f32), ((packed, half), i16)], kept, got
    )
    got = zhi_exchange(send, 3, 1)
    spread = ((ny, 3 * quarter, half), bf16)
    mine, to_y = call(swiglu_kernel, [((3 * quarter, half), bf16), spread], total, got)
    theirs = zhi_exchange(mine, 1, 3)
    first = lax.all_to_all(to_y, "y", 0, 0)
    (to_y,) = call(spread_kernel, [spread], theirs)
    second = lax.all_to_all(to_y, "y", 0, 0)

    def units(block):
        block = block.reshape(ny, 3, quarter, half)
        return block.transpose(1, 0, 2, 3).reshape(3, hidden_units, half)

    first, second = units(first), units(second)

    def back_of(side):
        return dot(side[1], gate_eff, ((0,), (0,))) + dot(side[2], up_eff, ((0,), (0,)))

    back_first, back_second = back_of(first), back_of(second)
    stays = jnp.where(own_kept, back_first, back_second)
    leaves = jnp.where(own_kept, back_second, back_first)
    back = stays + lax.ppermute(leaves, "core", swap)
    back = lax.all_to_all(back.reshape(nx, half // nx, width), "x", 0, 0).sum(axis=0)
    back = lax.all_to_all(back.reshape(nzlo, rows, width), "zlo", 0, 0).sum(axis=0)

    kept_side = jnp.where(own_kept, own, other)
    sent_side = jnp.where(own_kept, other, own)

    def weight_grad(member, side):
        return dot(first[member], kept_side[side], ((1,), (0,))) + dot(
            second[member], sent_side[side], ((1,), (0,))
        )

    grad_gate = jnp.where(gate_keep, weight_grad(1, 0), 0.0).astype(bf16)
    grad_up = jnp.where(up_keep, weight_grad(2, 0), 0.0).astype(bf16)
    grad_down = jnp.where(down_keep, weight_grad(0, 1), 0.0).astype(bf16)
    return (back.astype(bf16), grad_gate.T, grad_up.T, grad_down)


def solution(mesh):
    fine = Mesh(
        np.asarray(mesh.devices).reshape(4, 4, 8, 4, 2), ("zhi", "y", "zlo", "x", "core")
    )
    row, col = ("zhi", "y"), ("zlo", "x", "core")
    return jax.shard_map(
        body,
        mesh=fine,
        in_specs=(
            P(col, row),
            P(col, row),
            P(row, col),
            P(row, col),
            P(col, row),
            P(row, col),
            P(row, col),
            P(col, row),
        ),
        out_specs=(P(col, row), P(row, col), P(row, col), P(col, row)),
        check_vma=False,
    )
```

```python
import jax
import jax.numpy as jnp
import numpy as np
from jax import lax
from jax.experimental import pallas as pl
from jax.experimental.pallas import tpu as pltpu
from jax.sharding import Mesh, PartitionSpec as P

bf16 = jnp.bfloat16
f32 = jnp.float32
keep_sets = ((0, 1, 2), (0, 3, 4), (1, 3, 5), (2, 4, 5))


def keep_planes(pattern):
    planes = []
    for members in keep_sets:
        kept = pattern == members[0]
        for member in members[1:]:
            kept = kept | (pattern == member)
        planes.append(kept.astype(bf16))
    return planes


def spread_matrix(groups):
    row = lax.broadcasted_iota(jnp.int32, (4 * groups, 4 * groups), 0)
    col = lax.broadcasted_iota(jnp.int32, (4 * groups, 4 * groups), 1)
    return ((row % groups) * 4 + row // groups == col).astype(bf16)


def dot(a, b, dims):
    return lax.dot_general(a, b, (dims, ((), ())), preferred_element_type=f32)


def zhi_exchange(block, flip0, flip1):
    pairs = [
        (z * 2 + c, (z ^ (flip0, flip1)[c]) * 2 + c) for z in range(4) for c in range(2)
    ]
    return lax.ppermute(block, ("zhi", "core"), pairs)


EXTRA = 16
COST = 2 * 10**9


def pack(values):
    rows, powers = [], []
    for value in values:
        most = jnp.max(jnp.abs(value), axis=0, keepdims=True)
        power = jnp.ceil(jnp.log2(jnp.maximum(most, 1e-30))) - 14.0
        rows.append(to_int16(jnp.round(value * jnp.exp2(-power))))
        powers.append(power)
    spot = lax.broadcasted_iota(jnp.int32, (EXTRA, values[0].shape[1]), 0)
    tail = jnp.where(spot == 0, powers[0], jnp.where(spot == 1, powers[1], powers[2]))
    return rows, to_int16(tail)


def to_int16(values):
    return values.astype(jnp.int32).astype(jnp.int16)


def wide(block):
    return block.astype(jnp.int32).astype(f32)


def unpack(block, units):
    powers = wide(block[3 * units : 3 * units + EXTRA, :])
    return [
        wide(block[i * units : (i + 1) * units, :]) * jnp.exp2(powers[i : i + 1, :])
        for i in range(3)
    ]


def spread_kernel(block_ref, out_ref):
    for c in range(out_ref.shape[0]):
        out_ref[c] = block_ref[...]


def partial_kernel(flag_ref, gate_ref, up_ref, down_ref, own_ref, other_ref, out_ref):
    ny, units = out_ref.shape[0], gate_ref.shape[0] // out_ref.shape[0]
    is_own = flag_ref[0] == 1
    tokens = jnp.where(is_own, own_ref[0], other_ref[0])
    grad_out = jnp.where(is_own, own_ref[1], other_ref[1])
    products = [
        dot(gate_ref[...], tokens, ((1,), (1,))),
        dot(up_ref[...], tokens, ((1,), (1,))),
        dot(down_ref[...], grad_out, ((1,), (1,))),
    ]
    for c in range(ny):
        store([p[c * units : (c + 1) * units] for p in products], out_ref.at[c])


def store(values, send_ref):
    units = values[0].shape[0]
    rows, tail = pack(values)
    for i in range(3):
        send_ref[i * units : (i + 1) * units, :] = rows[i]
    send_ref[3 * units :, :] = tail


def sum_over_blocks(block_ref):
    units = (block_ref.shape[1] - EXTRA) // 3
    total = [0.0, 0.0, 0.0]
    for c in range(block_ref.shape[0]):
        parts = unpack(block_ref.at[c], units)
        total = [total[i] + parts[i] for i in range(3)]
    return total


def sent_sum_kernel(block_ref, send_ref):
    store(sum_over_blocks(block_ref), send_ref)


def kept_sum_kernel(block_ref, got_ref, total_ref, send_ref):
    total = sum_over_blocks(block_ref)
    parts = unpack(got_ref, total_ref.shape[1])
    total = [total[i] + parts[i] for i in range(3)]
    for i in range(3):
        total_ref[i] = total[i]
    store(total, send_ref)


def swiglu_kernel(total_ref, got_ref, out_ref, spread_ref):
    units = total_ref.shape[1]
    parts = unpack(got_ref, units)
    gate_pre, up_pre, hidden_grad = [total_ref[i] + parts[i] for i in range(3)]
    sigmoid_gate = jax.nn.sigmoid(gate_pre)
    silu_gate = gate_pre * sigmoid_gate
    results = (
        silu_gate * up_pre,
        hidden_grad * up_pre * sigmoid_gate * (1.0 + gate_pre * (1.0 - sigmoid_gate)),
        hidden_grad * silu_gate,
    )
    for i, result in enumerate(results):
        result = result.astype(bf16)
        out_ref[i * units : (i + 1) * units, :] = result
        for c in range(spread_ref.shape[0]):
            spread_ref[c, i * units : (i + 1) * units, :] = result


def back_product(block_ref, gate_ref, up_ref):
    ny, units = block_ref.shape[0], block_ref.shape[1] // 3

    def member(i):
        return jnp.concatenate(
            [block_ref[c, i * units : (i + 1) * units, :] for c in range(ny)], axis=0
        )

    return dot(member(1), gate_ref[...], ((0,), (0,))) + dot(
        member(2), up_ref[...], ((0,), (0,))
    )


def first_back_kernel(block_ref, gate_ref, up_ref, out_ref):
    out_ref[...] = back_product(block_ref, gate_ref, up_ref)


def second_back_kernel(flag_ref, first_ref, block_ref, gate_ref, up_ref, stays_ref, leaves_ref):
    first, second = first_ref[...], back_product(block_ref, gate_ref, up_ref)
    first_stays = flag_ref[0] == 1
    stays_ref[...] = jnp.where(first_stays, first, second)
    leaves_ref[...] = jnp.where(first_stays, second, first)


def core_sum_kernel(stays_ref, got_ref, send_ref):
    rows = send_ref.shape[1] - EXTRA
    for c in range(send_ref.shape[0]):
        part = slice(c * rows, (c + 1) * rows)
        value = stays_ref[part, :] + got_ref[part, :]
        most = jnp.max(jnp.abs(value), axis=0, keepdims=True)
        power = jnp.ceil(jnp.log2(jnp.maximum(most, 1e-30))) - 14.0
        send_ref[c, :rows, :] = to_int16(jnp.round(value * jnp.exp2(-power)))
        send_ref[c, rows:, :] = to_int16(jnp.broadcast_to(power, (EXTRA, value.shape[1])))


def x_sum_kernel(block_ref, out_ref):
    rows = block_ref.shape[1] - EXTRA
    total = 0.0
    for c in range(block_ref.shape[0]):
        powers = wide(block_ref[c, rows:, :])
        total = total + wide(block_ref[c, :rows, :]) * jnp.exp2(powers[:1, :])
    count, each = out_ref.shape[0], out_ref.shape[1]
    for c in range(count):
        out_ref[c] = total[c * each : (c + 1) * each]


def call(kernel, outs, *args, scalars=0):
    specs = [pl.BlockSpec(memory_space=pltpu.SMEM)] * scalars
    specs += [pl.BlockSpec()] * (len(args) - scalars)
    return pl.pallas_call(
        kernel,
        in_specs=specs,
        out_shape=[jax.ShapeDtypeStruct(shape, kind) for shape, kind in outs],
        compiler_params=pltpu.CompilerParams(vmem_limit_bytes=32 * 2**20),
        cost_estimate=pl.CostEstimate(flops=COST, bytes_accessed=1024, transcendentals=0),
    )(*args)


def body(inputs, cotangent, gate_weight, up_weight, down_weight, gate_pattern, up_pattern, down_pattern):
    sizes = {"zhi": 4, "y": 4, "zlo": 8, "x": 4, "core": 2}
    rows, width = inputs.shape
    hidden_units = down_weight.shape[0]
    half = rows * sizes["zlo"] * sizes["x"]
    ny = sizes["y"]
    quarter = hidden_units // ny
    spread_width = spread_matrix(width // 4)
    spread_units = spread_matrix(hidden_units // 4)
    gate_keep = dot(jnp.concatenate(keep_planes(gate_pattern.T), axis=1), spread_width, ((1,), (0,))) > 0.5
    up_keep = dot(jnp.concatenate(keep_planes(up_pattern.T), axis=1), spread_width, ((1,), (0,))) > 0.5
    down_keep = dot(spread_units, jnp.concatenate(keep_planes(down_pattern), axis=0), ((0,), (0,))) > 0.5
    zero = jnp.zeros((), bf16)
    gate_eff = jnp.where(gate_keep, gate_weight.T, zero)
    up_eff = jnp.where(up_keep, up_weight.T, zero)
    down_eff = jnp.where(down_keep, down_weight, zero)

    swap = [(0, 1), (1, 0)]
    nx, nzlo = sizes["x"], sizes["zlo"]
    both = jnp.stack([inputs, cotangent])
    both = jnp.broadcast_to(both[None], (nzlo, *both.shape))
    both = lax.all_to_all(both, "zlo", 0, 0)
    both, gate_eff, up_eff, down_eff = lax.optimization_barrier(
        (both, gate_eff, up_eff, down_eff)
    )
    (both,) = call(spread_kernel, [((nx, nzlo, 2, rows, width), bf16)], both)
    both = lax.all_to_all(both, "x", 0, 0)
    own = both.transpose(2, 0, 1, 3, 4).reshape(2, half, width)
    other = lax.ppermute(own, "core", swap)

    zhi, core = lax.axis_index("zhi"), lax.axis_index("core")
    keep = jnp.where(core == 0, (zhi ^ (zhi >> 1)) & 1, zhi >> 1)
    own_kept = keep == core
    flag = own_kept.astype(jnp.int32).reshape(1)

    i16 = jnp.int16
    packed = 3 * quarter + EXTRA
    block = [((ny, packed, half), i16)]
    operands = (gate_eff, up_eff, down_eff, own, other)
    (sent,) = call(partial_kernel, block, 1 - flag, *operands, scalars=1)
    (kept,) = call(partial_kernel, block, flag, *operands, scalars=1)
    sent = lax.all_to_all(sent, "y", 0, 0)
    (send,) = call(sent_sum_kernel, [((packed, half), i16)], sent)
    kept, send = lax.optimization_barrier((kept, send))
    got = zhi_exchange(send, 1, 3)
    kept = lax.all_to_all(kept, "y", 0, 0)
    total, send = call(
        kept_sum_kernel, [((3, quarter, half), f32), ((packed, half), i16)], kept, got
    )
    got = zhi_exchange(send, 3, 1)
    spread = ((ny, 3 * quarter, half), bf16)
    mine, to_y = call(swiglu_kernel, [((3 * quarter, half), bf16), spread], total, got)
    theirs = zhi_exchange(mine, 1, 3)
    first = lax.all_to_all(to_y, "y", 0, 0)
    (to_y,) = call(spread_kernel, [spread], theirs)
    second = lax.all_to_all(to_y, "y", 0, 0)

    (back_first,) = call(
        first_back_kernel, [((half, width), f32)], first, gate_eff, up_eff
    )
    stays, leaves = call(
        second_back_kernel,
        [((half, width), f32)] * 2,
        flag, back_first, second, gate_eff, up_eff,
        scalars=1,
    )
    got = lax.ppermute(leaves, "core", swap)
    (back,) = call(core_sum_kernel, [((nx, half // nx + EXTRA, width), i16)], stays, got)
    back, first, second = lax.optimization_barrier((back, first, second))
    back = lax.all_to_all(back, "x", 0, 0)
    (back,) = call(x_sum_kernel, [((nzlo, rows, width), f32)], back)
    back = lax.all_to_all(back, "zlo", 0, 0).sum(axis=0)

    def units(block):
        block = block.reshape(ny, 3, quarter, half)
        return block.transpose(1, 0, 2, 3).reshape(3, hidden_units, half)

    first, second = units(first), units(second)
    kept_side = jnp.where(own_kept, own, other)
    sent_side = jnp.where(own_kept, other, own)

    def weight_grad(member, side):
        return dot(first[member], kept_side[side], ((1,), (0,))) + dot(
            second[member], sent_side[side], ((1,), (0,))
        )

    grad_gate = jnp.where(gate_keep, weight_grad(1, 0), 0.0).astype(bf16)
    grad_up = jnp.where(up_keep, weight_grad(2, 0), 0.0).astype(bf16)
    grad_down = jnp.where(down_keep, weight_grad(0, 1), 0.0).astype(bf16)
    return (back.astype(bf16), grad_gate.T, grad_up.T, grad_down)


def solution(mesh):
    fine = Mesh(
        np.asarray(mesh.devices).reshape(4, 4, 8, 4, 2), ("zhi", "y", "zlo", "x", "core")
    )
    row, col = ("zhi", "y"), ("zlo", "x", "core")
    return jax.shard_map(
        body,
        mesh=fine,
        in_specs=(
            P(col, row),
            P(col, row),
            P(row, col),
            P(row, col),
            P(col, row),
            P(row, col),
            P(row, col),
            P(col, row),
        ),
        out_specs=(P(col, row), P(row, col), P(row, col), P(col, row)),
        check_vma=False,
    )
```

```python
import jax
import jax.numpy as jnp
import numpy as np
from jax import lax
from jax.experimental import pallas as pl
from jax.experimental.pallas import tpu as pltpu
from jax.sharding import Mesh, PartitionSpec as P

bf16 = jnp.bfloat16
f32 = jnp.float32
keep_sets = ((0, 1, 2), (0, 3, 4), (1, 3, 5), (2, 4, 5))


def keep_planes(pattern):
    planes = []
    for members in keep_sets:
        kept = pattern == members[0]
        for member in members[1:]:
            kept = kept | (pattern == member)
        planes.append(kept.astype(bf16))
    return planes


def spread_matrix(groups):
    row = lax.broadcasted_iota(jnp.int32, (4 * groups, 4 * groups), 0)
    col = lax.broadcasted_iota(jnp.int32, (4 * groups, 4 * groups), 1)
    return ((row % groups) * 4 + row // groups == col).astype(bf16)


def dot(a, b, dims):
    return lax.dot_general(a, b, (dims, ((), ())), preferred_element_type=f32)


def zhi_exchange(block, flip0, flip1):
    pairs = [
        (z * 2 + c, (z ^ (flip0, flip1)[c]) * 2 + c) for z in range(4) for c in range(2)
    ]
    return lax.ppermute(block, ("zhi", "core"), pairs)


EXTRA = 16
COST = 2 * 10**9


def pack(values):
    rows, powers = [], []
    for value in values:
        most = jnp.max(jnp.abs(value), axis=0, keepdims=True)
        power = jnp.ceil(jnp.log2(jnp.maximum(most, 1e-30))) - 14.0
        rows.append(to_int16(jnp.round(value * jnp.exp2(-power))))
        powers.append(power)
    spot = lax.broadcasted_iota(jnp.int32, (EXTRA, values[0].shape[1]), 0)
    tail = jnp.where(spot == 0, powers[0], jnp.where(spot == 1, powers[1], powers[2]))
    return rows, to_int16(tail)


def to_int16(values):
    return values.astype(jnp.int32).astype(jnp.int16)


def wide(block):
    return block.astype(jnp.int32).astype(f32)


def unpack(block, units):
    powers = wide(block[3 * units : 3 * units + EXTRA, :])
    return [
        wide(block[i * units : (i + 1) * units, :]) * jnp.exp2(powers[i : i + 1, :])
        for i in range(3)
    ]


def spread_kernel(block_ref, out_ref):
    for c in range(out_ref.shape[0]):
        out_ref[c] = block_ref[...]


def partial_kernel(flag_ref, gate_ref, up_ref, down_ref, own_ref, other_ref, out_ref):
    ny, units = out_ref.shape[0], gate_ref.shape[0] // out_ref.shape[0]
    half = own_ref.shape[1]
    own_front = flag_ref[0] == 1
    for spot, (a_ref, b_ref) in enumerate(((own_ref, other_ref), (other_ref, own_ref))):
        tokens = jnp.where(own_front, a_ref[0], b_ref[0])
        grad_out = jnp.where(own_front, a_ref[1], b_ref[1])
        products = [
            dot(gate_ref[...], tokens, ((1,), (1,))),
            dot(up_ref[...], tokens, ((1,), (1,))),
            dot(down_ref[...], grad_out, ((1,), (1,))),
        ]
        for c in range(ny):
            store(
                [p[c * units : (c + 1) * units] for p in products],
                out_ref.at[c, :, spot * half : (spot + 1) * half],
            )


def store(values, send_ref):
    units = values[0].shape[0]
    rows, tail = pack(values)
    for i in range(3):
        send_ref[i * units : (i + 1) * units, :] = rows[i]
    send_ref[3 * units :, :] = tail


def sum_over_blocks(block_ref):
    units = (block_ref.shape[1] - EXTRA) // 3
    total = [0.0, 0.0, 0.0]
    for c in range(block_ref.shape[0]):
        parts = unpack(block_ref.at[c], units)
        total = [total[i] + parts[i] for i in range(3)]
    return total


def first_sum_kernel(block_ref, total_ref, send_ref):
    half = total_ref.shape[2]
    total = sum_over_blocks(block_ref.at[:, :, :half])
    for i in range(3):
        total_ref[i] = total[i]
    store(sum_over_blocks(block_ref.at[:, :, half:]), send_ref)


def next_sum_kernel(total_ref, got_ref, out_ref, send_ref):
    parts = unpack(got_ref, total_ref.shape[1])
    total = [total_ref[i] + parts[i] for i in range(3)]
    for i in range(3):
        out_ref[i] = total[i]
    store(total, send_ref)


def swiglu_kernel(total_ref, got_ref, out_ref):
    units = total_ref.shape[1]
    parts = unpack(got_ref, units)
    gate_pre, up_pre, hidden_grad = [total_ref[i] + parts[i] for i in range(3)]
    sigmoid_gate = jax.nn.sigmoid(gate_pre)
    silu_gate = gate_pre * sigmoid_gate
    results = (
        silu_gate * up_pre,
        hidden_grad * up_pre * sigmoid_gate * (1.0 + gate_pre * (1.0 - sigmoid_gate)),
        hidden_grad * silu_gate,
    )
    for i, result in enumerate(results):
        out_ref[i * units : (i + 1) * units, :] = result.astype(bf16)


def back_product(block_ref, gate_ref, up_ref):
    ny, units = block_ref.shape[0], block_ref.shape[1] // 3

    def member(i):
        return jnp.concatenate(
            [block_ref[c, i * units : (i + 1) * units, :] for c in range(ny)], axis=0
        )

    return dot(member(1), gate_ref[...], ((0,), (0,))) + dot(
        member(2), up_ref[...], ((0,), (0,))
    )


def first_back_kernel(block_ref, gate_ref, up_ref, out_ref):
    out_ref[...] = back_product(block_ref, gate_ref, up_ref)


def second_back_kernel(flag_ref, first_ref, block_ref, gate_ref, up_ref, stays_ref, leaves_ref):
    first, second = first_ref[...], back_product(block_ref, gate_ref, up_ref)
    first_stays = flag_ref[0] == 1
    stays_ref[...] = jnp.where(first_stays, first, second)
    leaves_ref[...] = jnp.where(first_stays, second, first)


def core_sum_kernel(stays_ref, got_ref, send_ref):
    rows = send_ref.shape[1] - EXTRA
    for c in range(send_ref.shape[0]):
        part = slice(c * rows, (c + 1) * rows)
        value = stays_ref[part, :] + got_ref[part, :]
        most = jnp.max(jnp.abs(value), axis=0, keepdims=True)
        power = jnp.ceil(jnp.log2(jnp.maximum(most, 1e-30))) - 14.0
        send_ref[c, :rows, :] = to_int16(jnp.round(value * jnp.exp2(-power)))
        send_ref[c, rows:, :] = to_int16(jnp.broadcast_to(power, (EXTRA, value.shape[1])))


def x_sum_kernel(block_ref, out_ref):
    rows = block_ref.shape[1] - EXTRA
    total = 0.0
    for c in range(block_ref.shape[0]):
        powers = wide(block_ref[c, rows:, :])
        total = total + wide(block_ref[c, :rows, :]) * jnp.exp2(powers[:1, :])
    count, each = out_ref.shape[0], out_ref.shape[1]
    for c in range(count):
        out_ref[c] = total[c * each : (c + 1) * each]


def call(kernel, outs, *args, scalars=0):
    specs = [pl.BlockSpec(memory_space=pltpu.SMEM)] * scalars
    specs += [pl.BlockSpec()] * (len(args) - scalars)
    return pl.pallas_call(
        kernel,
        in_specs=specs,
        out_shape=[jax.ShapeDtypeStruct(shape, kind) for shape, kind in outs],
        compiler_params=pltpu.CompilerParams(vmem_limit_bytes=32 * 2**20),
        cost_estimate=pl.CostEstimate(flops=COST, bytes_accessed=1024, transcendentals=0),
    )(*args)


def body(inputs, cotangent, gate_weight, up_weight, down_weight, gate_pattern, up_pattern, down_pattern):
    sizes = {"zhi": 4, "y": 4, "zlo": 8, "x": 4, "core": 2}
    rows, width = inputs.shape
    hidden_units = down_weight.shape[0]
    half = rows * sizes["zlo"] * sizes["x"]
    ny = sizes["y"]
    quarter = hidden_units // ny
    spread_width = spread_matrix(width // 4)
    spread_units = spread_matrix(hidden_units // 4)
    gate_keep = dot(jnp.concatenate(keep_planes(gate_pattern.T), axis=1), spread_width, ((1,), (0,))) > 0.5
    up_keep = dot(jnp.concatenate(keep_planes(up_pattern.T), axis=1), spread_width, ((1,), (0,))) > 0.5
    down_keep = dot(spread_units, jnp.concatenate(keep_planes(down_pattern), axis=0), ((0,), (0,))) > 0.5
    zero = jnp.zeros((), bf16)
    gate_eff = jnp.where(gate_keep, gate_weight.T, zero)
    up_eff = jnp.where(up_keep, up_weight.T, zero)
    down_eff = jnp.where(down_keep, down_weight, zero)

    swap = [(0, 1), (1, 0)]
    nx, nzlo = sizes["x"], sizes["zlo"]
    both = jnp.stack([inputs, cotangent])
    both = jnp.broadcast_to(both[None], (nzlo, *both.shape))
    both = lax.all_to_all(both, "zlo", 0, 0)
    both, gate_eff, up_eff, down_eff = lax.optimization_barrier(
        (both, gate_eff, up_eff, down_eff)
    )
    (both,) = call(spread_kernel, [((nx, nzlo, 2, rows, width), bf16)], both)
    both = lax.all_to_all(both, "x", 0, 0)
    own = both.transpose(2, 0, 1, 3, 4).reshape(2, half, width)
    other = lax.ppermute(own, "core", swap)

    zhi, core = lax.axis_index("zhi"), lax.axis_index("core")
    keep = jnp.where(core == 0, (zhi ^ (zhi >> 1)) & 1, zhi >> 1)
    own_kept = keep == core
    flag = own_kept.astype(jnp.int32).reshape(1)

    i16 = jnp.int16
    packed = 3 * quarter + EXTRA
    (block,) = call(
        partial_kernel,
        [((ny, packed, 2 * half), i16)],
        flag, gate_eff, up_eff, down_eff, own, other,
        scalars=1,
    )
    block = lax.all_to_all(block, "y", 0, 0)
    pair = [((3, quarter, half), f32), ((packed, half), i16)]
    total, send = call(first_sum_kernel, pair, block)
    got = zhi_exchange(send, 1, 3)
    total, send = call(next_sum_kernel, pair, total, got)
    got = zhi_exchange(send, 3, 1)
    (mine,) = call(swiglu_kernel, [((3 * quarter, half), bf16)], total, got)
    theirs = zhi_exchange(mine, 1, 3)
    spread = [((ny, 3 * quarter, half), bf16)]
    (to_y,) = call(spread_kernel, spread, mine)
    first = lax.all_to_all(to_y, "y", 0, 0)
    (to_y,) = call(spread_kernel, spread, theirs)
    second = lax.all_to_all(to_y, "y", 0, 0)

    (back_first,) = call(
        first_back_kernel, [((half, width), f32)], first, gate_eff, up_eff
    )
    stays, leaves = call(
        second_back_kernel,
        [((half, width), f32)] * 2,
        flag, back_first, second, gate_eff, up_eff,
        scalars=1,
    )
    got = lax.ppermute(leaves, "core", swap)
    (back,) = call(core_sum_kernel, [((nx, half // nx + EXTRA, width), i16)], stays, got)
    back, first, second = lax.optimization_barrier((back, first, second))
    back = lax.all_to_all(back, "x", 0, 0)
    (back,) = call(x_sum_kernel, [((nzlo, rows, width), f32)], back)
    back = lax.all_to_all(back, "zlo", 0, 0).sum(axis=0)

    def units(block):
        block = block.reshape(ny, 3, quarter, half)
        return block.transpose(1, 0, 2, 3).reshape(3, hidden_units, half)

    first, second = units(first), units(second)
    kept_side = jnp.where(own_kept, own, other)
    sent_side = jnp.where(own_kept, other, own)

    def weight_grad(member, side):
        return dot(first[member], kept_side[side], ((1,), (0,))) + dot(
            second[member], sent_side[side], ((1,), (0,))
        )

    grad_gate = jnp.where(gate_keep, weight_grad(1, 0), 0.0).astype(bf16)
    grad_up = jnp.where(up_keep, weight_grad(2, 0), 0.0).astype(bf16)
    grad_down = jnp.where(down_keep, weight_grad(0, 1), 0.0).astype(bf16)
    return (back.astype(bf16), grad_gate.T, grad_up.T, grad_down)


def solution(mesh):
    fine = Mesh(
        np.asarray(mesh.devices).reshape(4, 4, 8, 4, 2), ("zhi", "y", "zlo", "x", "core")
    )
    row, col = ("zhi", "y"), ("zlo", "x", "core")
    return jax.shard_map(
        body,
        mesh=fine,
        in_specs=(
            P(col, row),
            P(col, row),
            P(row, col),
            P(row, col),
            P(col, row),
            P(row, col),
            P(row, col),
            P(col, row),
        ),
        out_specs=(P(col, row), P(row, col), P(row, col), P(col, row)),
        check_vma=False,
    )
```

```python
import jax
import jax.numpy as jnp
import numpy as np
from jax import lax
from jax.experimental import pallas as pl
from jax.experimental.pallas import tpu as pltpu
from jax.sharding import Mesh, PartitionSpec as P

bf16 = jnp.bfloat16
f32 = jnp.float32
keep_sets = ((0, 1, 2), (0, 3, 4), (1, 3, 5), (2, 4, 5))


def keep_planes(pattern, axis):
    planes = []
    for members in keep_sets:
        kept = pattern == members[0]
        for member in members[1:]:
            kept = kept | (pattern == member)
        planes.append(jnp.where(kept, 1.0, 0.0).astype(bf16))
    return jnp.concatenate(planes, axis=axis)


def spread_matrix(size, axis):
    place = lax.broadcasted_iota(jnp.int32, (size, size), axis)
    source = lax.broadcasted_iota(jnp.int32, (size, size), 1 - axis)
    moved = (place >> 2) + (place & 3) * (size // 4) == source
    return jnp.where(moved, 1.0, 0.0).astype(bf16)


def dot(a, b, dims):
    return lax.dot_general(a, b, (dims, ((), ())), preferred_element_type=f32)


def zhi_exchange(block, flip0, flip1):
    pairs = [
        (z * 2 + c, (z ^ (flip0, flip1)[c]) * 2 + c) for z in range(4) for c in range(2)
    ]
    return lax.ppermute(block, ("zhi", "core"), pairs)


EXTRA = 16
COST = 2 * 10**9


def pack(values):
    rows, powers = [], []
    for value in values:
        most = jnp.max(jnp.abs(value), axis=0, keepdims=True)
        power = jnp.ceil(jnp.log2(jnp.maximum(most, 1e-30))) - 14.0
        rows.append(to_int16(jnp.round(value * jnp.exp2(-power))))
        powers.append(power)
    spot = lax.broadcasted_iota(jnp.int32, (EXTRA, values[0].shape[1]), 0)
    tail = jnp.where(spot == 0, powers[0], jnp.where(spot == 1, powers[1], powers[2]))
    return rows, to_int16(tail)


def to_int16(values):
    return values.astype(jnp.int32).astype(jnp.int16)


def wide(block):
    return block.astype(jnp.int32).astype(f32)


def unpack(block, units):
    powers = wide(block[3 * units : 3 * units + EXTRA, :])
    return [
        wide(block[i * units : (i + 1) * units, :]) * jnp.exp2(powers[i : i + 1, :])
        for i in range(3)
    ]


def mask_kernel(*refs):
    patterns, weights, kept, masks = refs[:3], refs[3:6], refs[6:9], refs[9:]
    units, width = weights[0].shape
    across, down = spread_matrix(width, 1), spread_matrix(units, 0)
    for i in range(3):
        if i < 2:
            mask = dot(keep_planes(patterns[i][...], 1), across, ((1,), (0,)))
        else:
            mask = dot(down, keep_planes(patterns[i][...], 0), ((1,), (0,)))
        masks[i][...] = mask.astype(bf16)
        kept[i][...] = jnp.where(mask > 0.5, weights[i][...].astype(f32), 0.0).astype(bf16)


def spread_kernel(block_ref, out_ref):
    for c in range(out_ref.shape[0]):
        out_ref[c] = block_ref[...]


def partial_kernel(flag_ref, gate_ref, up_ref, down_ref, own_ref, other_ref, out_ref):
    ny, units = out_ref.shape[0], gate_ref.shape[0] // out_ref.shape[0]
    is_own = flag_ref[0] == 1
    tokens = jnp.where(is_own, own_ref[0], other_ref[0])
    grad_out = jnp.where(is_own, own_ref[1], other_ref[1])
    products = [
        dot(gate_ref[...], tokens, ((1,), (1,))),
        dot(up_ref[...], tokens, ((1,), (1,))),
        dot(down_ref[...], grad_out, ((1,), (1,))),
    ]
    for c in range(ny):
        store([p[c * units : (c + 1) * units] for p in products], out_ref.at[c])


def store(values, send_ref):
    units = values[0].shape[0]
    rows, tail = pack(values)
    for i in range(3):
        send_ref[i * units : (i + 1) * units, :] = rows[i]
    send_ref[3 * units :, :] = tail


def sum_over_blocks(block_ref):
    units = (block_ref.shape[1] - EXTRA) // 3
    total = [0.0, 0.0, 0.0]
    for c in range(block_ref.shape[0]):
        parts = unpack(block_ref.at[c], units)
        total = [total[i] + parts[i] for i in range(3)]
    return total


def sent_sum_kernel(block_ref, send_ref):
    store(sum_over_blocks(block_ref), send_ref)


def kept_sum_kernel(block_ref, got_ref, total_ref, send_ref):
    total = sum_over_blocks(block_ref)
    parts = unpack(got_ref, total_ref.shape[1])
    total = [total[i] + parts[i] for i in range(3)]
    for i in range(3):
        total_ref[i] = total[i]
    store(total, send_ref)


def swiglu_kernel(total_ref, got_ref, out_ref, spread_ref):
    units = total_ref.shape[1]
    parts = unpack(got_ref, units)
    gate_pre, up_pre, hidden_grad = [total_ref[i] + parts[i] for i in range(3)]
    sigmoid_gate = jax.nn.sigmoid(gate_pre)
    silu_gate = gate_pre * sigmoid_gate
    results = (
        silu_gate * up_pre,
        hidden_grad * up_pre * sigmoid_gate * (1.0 + gate_pre * (1.0 - sigmoid_gate)),
        hidden_grad * silu_gate,
    )
    for i, result in enumerate(results):
        result = result.astype(bf16)
        out_ref[i * units : (i + 1) * units, :] = result
        for c in range(spread_ref.shape[0]):
            spread_ref[c, i * units : (i + 1) * units, :] = result


def back_product(block_ref, gate_ref, up_ref):
    ny, units = block_ref.shape[0], block_ref.shape[1] // 3

    def member(i):
        return jnp.concatenate(
            [block_ref[c, i * units : (i + 1) * units, :] for c in range(ny)], axis=0
        )

    return dot(member(1), gate_ref[...], ((0,), (0,))) + dot(
        member(2), up_ref[...], ((0,), (0,))
    )


def back_kernel(flag_ref, first_ref, second_ref, gate_ref, up_ref, stays_ref, leaves_ref):
    first = back_product(first_ref, gate_ref, up_ref)
    second = back_product(second_ref, gate_ref, up_ref)
    first_stays = flag_ref[0] == 1
    stays_ref[...] = jnp.where(first_stays, first, second)
    leaves_ref[...] = jnp.where(first_stays, second, first)


def core_sum_kernel(stays_ref, got_ref, send_ref):
    rows = send_ref.shape[1] - EXTRA
    for c in range(send_ref.shape[0]):
        part = slice(c * rows, (c + 1) * rows)
        value = stays_ref[part, :] + got_ref[part, :]
        most = jnp.max(jnp.abs(value), axis=0, keepdims=True)
        power = jnp.ceil(jnp.log2(jnp.maximum(most, 1e-30))) - 14.0
        send_ref[c, :rows, :] = to_int16(jnp.round(value * jnp.exp2(-power)))
        send_ref[c, rows:, :] = to_int16(jnp.broadcast_to(power, (EXTRA, value.shape[1])))


def x_sum_kernel(block_ref, out_ref):
    rows = block_ref.shape[1] - EXTRA
    total = 0.0
    for c in range(block_ref.shape[0]):
        powers = wide(block_ref[c, rows:, :])
        total = total + wide(block_ref[c, :rows, :]) * jnp.exp2(powers[:1, :])
    count, each = out_ref.shape[0], out_ref.shape[1]
    for c in range(count):
        out_ref[c] = total[c * each : (c + 1) * each]


def last_sum_kernel(block_ref, out_ref):
    total = block_ref[0]
    for c in range(1, block_ref.shape[0]):
        total = total + block_ref[c]
    out_ref[...] = total.astype(bf16)


def call(kernel, outs, *args, scalars=0):
    specs = [pl.BlockSpec(memory_space=pltpu.SMEM)] * scalars
    specs += [pl.BlockSpec()] * (len(args) - scalars)
    return pl.pallas_call(
        kernel,
        in_specs=specs,
        out_shape=[jax.ShapeDtypeStruct(shape, kind) for shape, kind in outs],
        compiler_params=pltpu.CompilerParams(vmem_limit_bytes=32 * 2**20),
        cost_estimate=pl.CostEstimate(flops=COST, bytes_accessed=1024, transcendentals=0),
    )(*args)


def body(inputs, cotangent, gate_weight, up_weight, down_weight, gate_pattern, up_pattern, down_pattern):
    sizes = {"zhi": 4, "y": 4, "zlo": 8, "x": 4, "core": 2}
    rows, width = inputs.shape
    hidden_units = down_weight.shape[0]
    half = rows * sizes["zlo"] * sizes["x"]
    ny = sizes["y"]
    quarter = hidden_units // ny
    gate_eff, up_eff, down_eff, gate_mask, up_mask, down_mask = call(
        mask_kernel,
        [((hidden_units, width), bf16)] * 6,
        gate_pattern.T, up_pattern.T, down_pattern,
        gate_weight.T, up_weight.T, down_weight,
    )

    swap = [(0, 1), (1, 0)]
    nx, nzlo = sizes["x"], sizes["zlo"]
    both = jnp.stack([inputs, cotangent])
    both = jnp.broadcast_to(both[None], (nzlo, *both.shape))
    both = lax.all_to_all(both, "zlo", 0, 0)
    both, gate_eff, up_eff, down_eff = lax.optimization_barrier(
        (both, gate_eff, up_eff, down_eff)
    )
    (both,) = call(spread_kernel, [((nx, nzlo, 2, rows, width), bf16)], both)
    both = lax.all_to_all(both, "x", 0, 0)
    own = both.transpose(2, 0, 1, 3, 4).reshape(2, half, width)
    other = lax.ppermute(own, "core", swap)

    zhi, core = lax.axis_index("zhi"), lax.axis_index("core")
    keep = jnp.where(core == 0, (zhi ^ (zhi >> 1)) & 1, zhi >> 1)
    own_kept = keep == core
    flag = own_kept.astype(jnp.int32).reshape(1)

    i16 = jnp.int16
    packed = 3 * quarter + EXTRA
    block = [((ny, packed, half), i16)]
    operands = (gate_eff, up_eff, down_eff, own, other)
    (sent,) = call(partial_kernel, block, 1 - flag, *operands, scalars=1)
    (kept,) = call(partial_kernel, block, flag, *operands, scalars=1)
    sent = lax.all_to_all(sent, "y", 0, 0)
    (send,) = call(sent_sum_kernel, [((packed, half), i16)], sent)
    kept, send = lax.optimization_barrier((kept, send))
    got = zhi_exchange(send, 1, 3)
    kept = lax.all_to_all(kept, "y", 0, 0)
    total, send = call(
        kept_sum_kernel, [((3, quarter, half), f32), ((packed, half), i16)], kept, got
    )
    got = zhi_exchange(send, 3, 1)
    spread = ((ny, 3 * quarter, half), bf16)
    mine, to_y = call(swiglu_kernel, [((3 * quarter, half), bf16), spread], total, got)
    theirs = zhi_exchange(mine, 1, 3)
    first = lax.all_to_all(to_y, "y", 0, 0)
    (to_y,) = call(spread_kernel, [spread], theirs)
    second = lax.all_to_all(to_y, "y", 0, 0)

    stays, leaves = call(
        back_kernel,
        [((half, width), f32)] * 2,
        flag, first, second, gate_eff, up_eff,
        scalars=1,
    )
    got = lax.ppermute(leaves, "core", swap)
    (back,) = call(core_sum_kernel, [((nx, half // nx + EXTRA, width), i16)], stays, got)
    back, first, second = lax.optimization_barrier((back, first, second))
    back = lax.all_to_all(back, "x", 0, 0)
    (back,) = call(x_sum_kernel, [((nzlo, rows, width), f32)], back)
    back = lax.all_to_all(back, "zlo", 0, 0)
    (back,) = call(last_sum_kernel, [((rows, width), bf16)], back)

    def units(block):
        block = block.reshape(ny, 3, quarter, half)
        return block.transpose(1, 0, 2, 3).reshape(3, hidden_units, half)

    first, second = units(first), units(second)
    kept_side = jnp.where(own_kept, own, other)
    sent_side = jnp.where(own_kept, other, own)

    def weight_grad(member, side):
        return dot(first[member], kept_side[side], ((1,), (0,))) + dot(
            second[member], sent_side[side], ((1,), (0,))
        )

    grad_gate = jnp.where(gate_mask > 0.5, weight_grad(1, 0), 0.0).astype(bf16)
    grad_up = jnp.where(up_mask > 0.5, weight_grad(2, 0), 0.0).astype(bf16)
    grad_down = jnp.where(down_mask > 0.5, weight_grad(0, 1), 0.0).astype(bf16)
    return (back, grad_gate.T, grad_up.T, grad_down)


def solution(mesh):
    fine = Mesh(
        np.asarray(mesh.devices).reshape(4, 4, 8, 4, 2), ("zhi", "y", "zlo", "x", "core")
    )
    row, col = ("zhi", "y"), ("zlo", "x", "core")
    return jax.shard_map(
        body,
        mesh=fine,
        in_specs=(
            P(col, row),
            P(col, row),
            P(row, col),
            P(row, col),
            P(col, row),
            P(row, col),
            P(row, col),
            P(col, row),
        ),
        out_specs=(P(col, row), P(row, col), P(row, col), P(col, row)),
        check_vma=False,
    )
```

```python
import jax
import jax.numpy as jnp
import numpy as np
from jax import lax
from jax.experimental import pallas as pl
from jax.experimental.pallas import tpu as pltpu
from jax.sharding import Mesh, PartitionSpec as P

bf16 = jnp.bfloat16
f32 = jnp.float32
keep_sets = ((0, 1, 2), (0, 3, 4), (1, 3, 5), (2, 4, 5))


def keep_planes(pattern, axis):
    planes = []
    for members in keep_sets:
        kept = pattern == members[0]
        for member in members[1:]:
            kept = kept | (pattern == member)
        planes.append(jnp.where(kept, 1.0, 0.0).astype(bf16))
    return jnp.concatenate(planes, axis=axis)


def spread_matrix(size, axis):
    place = lax.broadcasted_iota(jnp.int32, (size, size), axis)
    source = lax.broadcasted_iota(jnp.int32, (size, size), 1 - axis)
    moved = (place >> 2) + (place & 3) * (size // 4) == source
    return jnp.where(moved, 1.0, 0.0).astype(bf16)


def dot(a, b, dims):
    return lax.dot_general(a, b, (dims, ((), ())), preferred_element_type=f32)


def zhi_exchange(block, flip0, flip1):
    pairs = [
        (z * 2 + c, (z ^ (flip0, flip1)[c]) * 2 + c) for z in range(4) for c in range(2)
    ]
    return lax.ppermute(block, ("zhi", "core"), pairs)


EXTRA = 16
COST = 2 * 10**9


def pack(values):
    rows, powers = [], []
    for value in values:
        most = jnp.max(jnp.abs(value), axis=0, keepdims=True)
        power = jnp.ceil(jnp.log2(jnp.maximum(most, 1e-30))) - 14.0
        rows.append(to_int16(jnp.round(value * jnp.exp2(-power))))
        powers.append(power)
    spot = lax.broadcasted_iota(jnp.int32, (EXTRA, values[0].shape[1]), 0)
    tail = jnp.where(spot == 0, powers[0], jnp.where(spot == 1, powers[1], powers[2]))
    return rows, to_int16(tail)


def to_int16(values):
    return values.astype(jnp.int32).astype(jnp.int16)


def wide(block):
    return block.astype(jnp.int32).astype(f32)


def unpack(block, units):
    powers = wide(block[3 * units : 3 * units + EXTRA, :])
    return [
        wide(block[i * units : (i + 1) * units, :]) * jnp.exp2(powers[i : i + 1, :])
        for i in range(3)
    ]


def mask_kernel(*refs):
    patterns, weights, kept, masks = refs[:3], refs[3:6], refs[6:9], refs[9:]
    units, width = weights[0].shape
    across, down = spread_matrix(width, 1), spread_matrix(units, 0)
    for i in range(3):
        if i < 2:
            mask = dot(keep_planes(patterns[i][...], 1), across, ((1,), (0,)))
        else:
            mask = dot(down, keep_planes(patterns[i][...], 0), ((1,), (0,)))
        masks[i][...] = mask.astype(bf16)
        kept[i][...] = jnp.where(mask > 0.5, weights[i][...].astype(f32), 0.0).astype(bf16)


def spread_kernel(block_ref, out_ref):
    for c in range(out_ref.shape[0]):
        out_ref[c] = block_ref[...]


def partial_kernel(flag_ref, gate_ref, up_ref, down_ref, own_ref, other_ref, out_ref):
    ny, units = out_ref.shape[0], gate_ref.shape[0] // out_ref.shape[0]
    is_own = flag_ref[0] == 1
    tokens = jnp.where(is_own, own_ref[0], other_ref[0])
    grad_out = jnp.where(is_own, own_ref[1], other_ref[1])
    products = [
        dot(gate_ref[...], tokens, ((1,), (1,))),
        dot(up_ref[...], tokens, ((1,), (1,))),
        dot(down_ref[...], grad_out, ((1,), (1,))),
    ]
    for c in range(ny):
        store([p[c * units : (c + 1) * units] for p in products], out_ref.at[c])


def store(values, send_ref):
    units = values[0].shape[0]
    rows, tail = pack(values)
    for i in range(3):
        send_ref[i * units : (i + 1) * units, :] = rows[i]
    send_ref[3 * units :, :] = tail


def sum_over_blocks(block_ref):
    units = (block_ref.shape[1] - EXTRA) // 3
    total = [0.0, 0.0, 0.0]
    for c in range(block_ref.shape[0]):
        parts = unpack(block_ref.at[c], units)
        total = [total[i] + parts[i] for i in range(3)]
    return total


def sent_sum_kernel(block_ref, send_ref):
    store(sum_over_blocks(block_ref), send_ref)


def kept_sum_kernel(block_ref, got_ref, total_ref, send_ref):
    total = sum_over_blocks(block_ref)
    parts = unpack(got_ref, total_ref.shape[1])
    total = [total[i] + parts[i] for i in range(3)]
    for i in range(3):
        total_ref[i] = total[i]
    store(total, send_ref)


def swiglu_kernel(total_ref, got_ref, out_ref, spread_ref):
    units = total_ref.shape[1]
    parts = unpack(got_ref, units)
    gate_pre, up_pre, hidden_grad = [total_ref[i] + parts[i] for i in range(3)]
    sigmoid_gate = jax.nn.sigmoid(gate_pre)
    silu_gate = gate_pre * sigmoid_gate
    results = (
        silu_gate * up_pre,
        hidden_grad * up_pre * sigmoid_gate * (1.0 + gate_pre * (1.0 - sigmoid_gate)),
        hidden_grad * silu_gate,
    )
    for i, result in enumerate(results):
        result = result.astype(bf16)
        out_ref[i * units : (i + 1) * units, :] = result
        for c in range(spread_ref.shape[0]):
            spread_ref[c, i * units : (i + 1) * units, :] = result


def back_product(block_ref, gate_ref, up_ref):
    ny, units = block_ref.shape[0], block_ref.shape[1] // 3

    def member(i):
        return jnp.concatenate(
            [block_ref[c, i * units : (i + 1) * units, :] for c in range(ny)], axis=0
        )

    return dot(member(1), gate_ref[...], ((0,), (0,))) + dot(
        member(2), up_ref[...], ((0,), (0,))
    )


def back_kernel(flag_ref, first_ref, second_ref, gate_ref, up_ref, stays_ref, leaves_ref):
    first = back_product(first_ref, gate_ref, up_ref)
    second = back_product(second_ref, gate_ref, up_ref)
    first_stays = flag_ref[0] == 1
    stays_ref[...] = jnp.where(first_stays, first, second)
    leaves_ref[...] = jnp.where(first_stays, second, first)


def core_sum_kernel(stays_ref, got_ref, send_ref):
    rows = send_ref.shape[1] - EXTRA
    for c in range(send_ref.shape[0]):
        part = slice(c * rows, (c + 1) * rows)
        value = stays_ref[part, :] + got_ref[part, :]
        most = jnp.max(jnp.abs(value), axis=0, keepdims=True)
        power = jnp.ceil(jnp.log2(jnp.maximum(most, 1e-30))) - 14.0
        send_ref[c, :rows, :] = to_int16(jnp.round(value * jnp.exp2(-power)))
        send_ref[c, rows:, :] = to_int16(jnp.broadcast_to(power, (EXTRA, value.shape[1])))


def x_sum_kernel(block_ref, out_ref):
    rows = block_ref.shape[1] - EXTRA
    total = 0.0
    for c in range(block_ref.shape[0]):
        powers = wide(block_ref[c, rows:, :])
        total = total + wide(block_ref[c, :rows, :]) * jnp.exp2(powers[:1, :])
    count, each = out_ref.shape[0], out_ref.shape[1]
    for c in range(count):
        out_ref[c] = total[c * each : (c + 1) * each]


def last_sum_kernel(block_ref, out_ref):
    total = block_ref[0]
    for c in range(1, block_ref.shape[0]):
        total = total + block_ref[c]
    out_ref[...] = total.astype(bf16)


def call(kernel, outs, *args, scalars=0):
    specs = [pl.BlockSpec(memory_space=pltpu.SMEM)] * scalars
    specs += [pl.BlockSpec()] * (len(args) - scalars)
    return pl.pallas_call(
        kernel,
        in_specs=specs,
        out_shape=[jax.ShapeDtypeStruct(shape, kind) for shape, kind in outs],
        compiler_params=pltpu.CompilerParams(vmem_limit_bytes=32 * 2**20),
        cost_estimate=pl.CostEstimate(flops=COST, bytes_accessed=1024, transcendentals=0),
    )(*args)


def body(inputs, cotangent, gate_weight, up_weight, down_weight, gate_pattern, up_pattern, down_pattern):
    sizes = {"zhi": 4, "y": 4, "zlo": 8, "x": 4, "core": 2}
    rows, width = inputs.shape
    hidden_units = down_weight.shape[0]
    half = rows * sizes["zlo"] * sizes["x"]
    ny = sizes["y"]
    quarter = hidden_units // ny
    swap = [(0, 1), (1, 0)]
    nx, nzlo = sizes["x"], sizes["zlo"]
    both = jnp.stack([inputs, cotangent])
    both = jnp.broadcast_to(both[None], (nzlo, *both.shape))
    both = lax.all_to_all(both, "zlo", 0, 0)
    both, gate_pattern, up_pattern, down_pattern = lax.optimization_barrier(
        (both, gate_pattern, up_pattern, down_pattern)
    )
    (both,) = call(spread_kernel, [((nx, nzlo, 2, rows, width), bf16)], both)
    both = lax.all_to_all(both, "x", 0, 0)

    gate_eff, up_eff, down_eff, gate_mask, up_mask, down_mask = call(
        mask_kernel,
        [((hidden_units, width), bf16)] * 6,
        gate_pattern.T, up_pattern.T, down_pattern,
        gate_weight.T, up_weight.T, down_weight,
    )

    both, gate_eff, up_eff, down_eff = lax.optimization_barrier(
        (both, gate_eff, up_eff, down_eff)
    )
    own = both.transpose(2, 0, 1, 3, 4).reshape(2, half, width)
    other = lax.ppermute(own, "core", swap)

    zhi, core = lax.axis_index("zhi"), lax.axis_index("core")
    keep = jnp.where(core == 0, (zhi ^ (zhi >> 1)) & 1, zhi >> 1)
    own_kept = keep == core
    flag = own_kept.astype(jnp.int32).reshape(1)

    i16 = jnp.int16
    packed = 3 * quarter + EXTRA
    block = [((ny, packed, half), i16)]
    operands = (gate_eff, up_eff, down_eff, own, other)
    (sent,) = call(partial_kernel, block, 1 - flag, *operands, scalars=1)
    (kept,) = call(partial_kernel, block, flag, *operands, scalars=1)
    sent = lax.all_to_all(sent, "y", 0, 0)
    (send,) = call(sent_sum_kernel, [((packed, half), i16)], sent)
    kept, send = lax.optimization_barrier((kept, send))
    got = zhi_exchange(send, 1, 3)
    kept = lax.all_to_all(kept, "y", 0, 0)
    total, send = call(
        kept_sum_kernel, [((3, quarter, half), f32), ((packed, half), i16)], kept, got
    )
    got = zhi_exchange(send, 3, 1)
    spread = ((ny, 3 * quarter, half), bf16)
    mine, to_y = call(swiglu_kernel, [((3 * quarter, half), bf16), spread], total, got)
    theirs = zhi_exchange(mine, 1, 3)
    first = lax.all_to_all(to_y, "y", 0, 0)
    (to_y,) = call(spread_kernel, [spread], theirs)
    second = lax.all_to_all(to_y, "y", 0, 0)

    stays, leaves = call(
        back_kernel,
        [((half, width), f32)] * 2,
        flag, first, second, gate_eff, up_eff,
        scalars=1,
    )
    got = lax.ppermute(leaves, "core", swap)
    (back,) = call(core_sum_kernel, [((nx, half // nx + EXTRA, width), i16)], stays, got)
    back, first, second = lax.optimization_barrier((back, first, second))
    back = lax.all_to_all(back, "x", 0, 0)
    (back,) = call(x_sum_kernel, [((nzlo, rows, width), f32)], back)
    back = lax.all_to_all(back, "zlo", 0, 0)
    (back,) = call(last_sum_kernel, [((rows, width), bf16)], back)

    def units(block):
        block = block.reshape(ny, 3, quarter, half)
        return block.transpose(1, 0, 2, 3).reshape(3, hidden_units, half)

    first, second = units(first), units(second)
    kept_side = jnp.where(own_kept, own, other)
    sent_side = jnp.where(own_kept, other, own)

    def weight_grad(member, side):
        return dot(first[member], kept_side[side], ((1,), (0,))) + dot(
            second[member], sent_side[side], ((1,), (0,))
        )

    grad_gate = jnp.where(gate_mask > 0.5, weight_grad(1, 0), 0.0).astype(bf16)
    grad_up = jnp.where(up_mask > 0.5, weight_grad(2, 0), 0.0).astype(bf16)
    grad_down = jnp.where(down_mask > 0.5, weight_grad(0, 1), 0.0).astype(bf16)
    return (back, grad_gate.T, grad_up.T, grad_down)


def solution(mesh):
    fine = Mesh(
        np.asarray(mesh.devices).reshape(4, 4, 8, 4, 2), ("zhi", "y", "zlo", "x", "core")
    )
    row, col = ("zhi", "y"), ("zlo", "x", "core")
    return jax.shard_map(
        body,
        mesh=fine,
        in_specs=(
            P(col, row),
            P(col, row),
            P(row, col),
            P(row, col),
            P(col, row),
            P(row, col),
            P(row, col),
            P(col, row),
        ),
        out_specs=(P(col, row), P(row, col), P(row, col), P(col, row)),
        check_vma=False,
    )
```

```python
import jax
import jax.numpy as jnp
import numpy as np
from jax import lax
from jax.experimental import pallas as pl
from jax.experimental.pallas import tpu as pltpu
from jax.sharding import Mesh, PartitionSpec as P

bf16 = jnp.bfloat16
f32 = jnp.float32
keep_sets = ((0, 1, 2), (0, 3, 4), (1, 3, 5), (2, 4, 5))


def keep_planes(pattern, axis):
    planes = []
    for members in keep_sets:
        kept = pattern == members[0]
        for member in members[1:]:
            kept = kept | (pattern == member)
        planes.append(jnp.where(kept, 1.0, 0.0).astype(bf16))
    return jnp.concatenate(planes, axis=axis)


def spread_matrix(size, axis):
    place = lax.broadcasted_iota(jnp.int32, (size, size), axis)
    source = lax.broadcasted_iota(jnp.int32, (size, size), 1 - axis)
    moved = (place >> 2) + (place & 3) * (size // 4) == source
    return jnp.where(moved, 1.0, 0.0).astype(bf16)


def dot(a, b, dims):
    return lax.dot_general(a, b, (dims, ((), ())), preferred_element_type=f32)


def zhi_exchange(block, flip0, flip1):
    pairs = [
        (z * 2 + c, (z ^ (flip0, flip1)[c]) * 2 + c) for z in range(4) for c in range(2)
    ]
    return lax.ppermute(block, ("zhi", "core"), pairs)


EXTRA = 16
COST = 2 * 10**9


def pack(values):
    rows, powers = [], []
    for value in values:
        most = jnp.max(jnp.abs(value), axis=0, keepdims=True)
        power = jnp.ceil(jnp.log2(jnp.maximum(most, 1e-30))) - 14.0
        rows.append(to_int16(jnp.round(value * jnp.exp2(-power))))
        powers.append(power)
    spot = lax.broadcasted_iota(jnp.int32, (EXTRA, values[0].shape[1]), 0)
    tail = jnp.where(spot == 0, powers[0], jnp.where(spot == 1, powers[1], powers[2]))
    return rows, to_int16(tail)


def to_int16(values):
    return values.astype(jnp.int32).astype(jnp.int16)


def wide(block):
    return block.astype(jnp.int32).astype(f32)


def unpack(block, units):
    powers = wide(block[3 * units : 3 * units + EXTRA, :])
    return [
        wide(block[i * units : (i + 1) * units, :]) * jnp.exp2(powers[i : i + 1, :])
        for i in range(3)
    ]


def mask_kernel(*refs):
    patterns, weights, kept, masks = refs[:3], refs[3:6], refs[6:9], refs[9:]
    units, width = weights[0].shape
    across, down = spread_matrix(width, 1), spread_matrix(units, 0)
    for i in range(3):
        if i < 2:
            mask = dot(keep_planes(patterns[i][...], 1), across, ((1,), (0,)))
        else:
            mask = dot(down, keep_planes(patterns[i][...], 0), ((1,), (0,)))
        masks[i][...] = mask.astype(bf16)
        kept[i][...] = jnp.where(mask > 0.5, weights[i][...].astype(f32), 0.0).astype(bf16)


def spread_kernel(block_ref, out_ref):
    for c in range(out_ref.shape[0]):
        out_ref[c] = block_ref[...]


def partial_kernel(flag_ref, gate_ref, up_ref, down_ref, own_ref, other_ref, out_ref):
    ny, units = out_ref.shape[0], gate_ref.shape[0] // out_ref.shape[0]
    is_own = flag_ref[0] == 1
    tokens = jnp.where(is_own, own_ref[0], other_ref[0])
    grad_out = jnp.where(is_own, own_ref[1], other_ref[1])
    products = [
        dot(gate_ref[...], tokens, ((1,), (1,))),
        dot(up_ref[...], tokens, ((1,), (1,))),
        dot(down_ref[...], grad_out, ((1,), (1,))),
    ]
    for c in range(ny):
        store([p[c * units : (c + 1) * units] for p in products], out_ref.at[c])


def store(values, send_ref):
    units = values[0].shape[0]
    rows, tail = pack(values)
    for i in range(3):
        send_ref[i * units : (i + 1) * units, :] = rows[i]
    send_ref[3 * units :, :] = tail


def sum_over_blocks(block_ref):
    units = (block_ref.shape[1] - EXTRA) // 3
    total = [0.0, 0.0, 0.0]
    for c in range(block_ref.shape[0]):
        parts = unpack(block_ref.at[c], units)
        total = [total[i] + parts[i] for i in range(3)]
    return total


def sent_sum_kernel(block_ref, send_ref):
    store(sum_over_blocks(block_ref), send_ref)


def kept_sum_kernel(block_ref, got_ref, total_ref, send_ref):
    total = sum_over_blocks(block_ref)
    parts = unpack(got_ref, total_ref.shape[1])
    total = [total[i] + parts[i] for i in range(3)]
    for i in range(3):
        total_ref[i] = total[i]
    store(total, send_ref)


def swiglu_kernel(total_ref, got_ref, out_ref, spread_ref):
    units = total_ref.shape[1]
    parts = unpack(got_ref, units)
    gate_pre, up_pre, hidden_grad = [total_ref[i] + parts[i] for i in range(3)]
    sigmoid_gate = jax.nn.sigmoid(gate_pre)
    silu_gate = gate_pre * sigmoid_gate
    results = (
        silu_gate * up_pre,
        hidden_grad * up_pre * sigmoid_gate * (1.0 + gate_pre * (1.0 - sigmoid_gate)),
        hidden_grad * silu_gate,
    )
    for i, result in enumerate(results):
        result = result.astype(bf16)
        out_ref[i * units : (i + 1) * units, :] = result
        for c in range(spread_ref.shape[0]):
            spread_ref[c, i * units : (i + 1) * units, :] = result


def back_product(block_ref, gate_ref, up_ref):
    ny, units = block_ref.shape[0], block_ref.shape[1] // 3

    def member(i):
        return jnp.concatenate(
            [block_ref[c, i * units : (i + 1) * units, :] for c in range(ny)], axis=0
        )

    return dot(member(1), gate_ref[...], ((0,), (0,))) + dot(
        member(2), up_ref[...], ((0,), (0,))
    )


def back_kernel(flag_ref, first_ref, second_ref, gate_ref, up_ref, stays_ref, leaves_ref):
    first = back_product(first_ref, gate_ref, up_ref)
    second = back_product(second_ref, gate_ref, up_ref)
    first_stays = flag_ref[0] == 1
    stays_ref[...] = jnp.where(first_stays, first, second)
    leaves_ref[...] = jnp.where(first_stays, second, first)


def core_sum_kernel(stays_ref, got_ref, send_ref):
    rows = send_ref.shape[1] - EXTRA
    for c in range(send_ref.shape[0]):
        part = slice(c * rows, (c + 1) * rows)
        value = stays_ref[part, :] + got_ref[part, :]
        most = jnp.max(jnp.abs(value), axis=0, keepdims=True)
        power = jnp.ceil(jnp.log2(jnp.maximum(most, 1e-30))) - 14.0
        send_ref[c, :rows, :] = to_int16(jnp.round(value * jnp.exp2(-power)))
        send_ref[c, rows:, :] = to_int16(jnp.broadcast_to(power, (EXTRA, value.shape[1])))


def x_sum_kernel(block_ref, out_ref):
    rows = block_ref.shape[1] - EXTRA
    total = 0.0
    for c in range(block_ref.shape[0]):
        powers = wide(block_ref[c, rows:, :])
        total = total + wide(block_ref[c, :rows, :]) * jnp.exp2(powers[:1, :])
    count, each = out_ref.shape[0], out_ref.shape[1]
    for c in range(count):
        out_ref[c] = total[c * each : (c + 1) * each]


def last_sum_kernel(block_ref, out_ref):
    total = block_ref[0]
    for c in range(1, block_ref.shape[0]):
        total = total + block_ref[c]
    out_ref[...] = total.astype(bf16)


def call(kernel, outs, *args, scalars=0, cost=COST):
    specs = [pl.BlockSpec(memory_space=pltpu.SMEM)] * scalars
    specs += [pl.BlockSpec()] * (len(args) - scalars)
    return pl.pallas_call(
        kernel,
        in_specs=specs,
        out_shape=[jax.ShapeDtypeStruct(shape, kind) for shape, kind in outs],
        compiler_params=pltpu.CompilerParams(vmem_limit_bytes=32 * 2**20),
        cost_estimate=pl.CostEstimate(flops=cost, bytes_accessed=1024, transcendentals=0),
    )(*args)


def body(inputs, cotangent, gate_weight, up_weight, down_weight, gate_pattern, up_pattern, down_pattern):
    sizes = {"zhi": 4, "y": 4, "zlo": 8, "x": 4, "core": 2}
    rows, width = inputs.shape
    hidden_units = down_weight.shape[0]
    half = rows * sizes["zlo"] * sizes["x"]
    ny = sizes["y"]
    quarter = hidden_units // ny
    swap = [(0, 1), (1, 0)]
    nx, nzlo = sizes["x"], sizes["zlo"]
    both = jnp.stack([inputs, cotangent])
    both = jnp.broadcast_to(both[None], (nzlo, *both.shape))
    both = lax.all_to_all(both, "zlo", 0, 0)
    both, gate_pattern, up_pattern, down_pattern = lax.optimization_barrier(
        (both, gate_pattern, up_pattern, down_pattern)
    )
    (both,) = call(spread_kernel, [((nx, nzlo, 2, rows, width), bf16)], both)
    both = lax.all_to_all(both, "x", 0, 0)

    gate_eff, up_eff, down_eff, gate_mask, up_mask, down_mask = call(
        mask_kernel,
        [((hidden_units, width), bf16)] * 6,
        gate_pattern.T, up_pattern.T, down_pattern,
        gate_weight.T, up_weight.T, down_weight,
    )

    both, gate_eff, up_eff, down_eff = lax.optimization_barrier(
        (both, gate_eff, up_eff, down_eff)
    )
    own = both.transpose(2, 0, 1, 3, 4).reshape(2, half, width)
    other = lax.ppermute(own, "core", swap)

    zhi, core = lax.axis_index("zhi"), lax.axis_index("core")
    keep = jnp.where(core == 0, (zhi ^ (zhi >> 1)) & 1, zhi >> 1)
    own_kept = keep == core
    flag = own_kept.astype(jnp.int32).reshape(1)

    i16 = jnp.int16
    packed = 3 * quarter + EXTRA
    block = [((ny, packed, half), i16)]
    operands = (gate_eff, up_eff, down_eff, own, other)
    (sent,) = call(partial_kernel, block, 1 - flag, *operands, scalars=1)
    (kept,) = call(partial_kernel, block, flag, *operands, scalars=1)
    sent = lax.all_to_all(sent, "y", 0, 0)
    (send,) = call(sent_sum_kernel, [((packed, half), i16)], sent)
    kept, send = lax.optimization_barrier((kept, send))
    got = zhi_exchange(send, 1, 3)
    kept = lax.all_to_all(kept, "y", 0, 0)
    total, send = call(
        kept_sum_kernel, [((3, quarter, half), f32), ((packed, half), i16)], kept, got
    )
    got = zhi_exchange(send, 3, 1)
    spread = ((ny, 3 * quarter, half), bf16)
    mine, to_y = call(swiglu_kernel, [((3 * quarter, half), bf16), spread], total, got)
    theirs = zhi_exchange(mine, 1, 3)
    first = lax.all_to_all(to_y, "y", 0, 0)
    (to_y,) = call(spread_kernel, [spread], theirs)
    second = lax.all_to_all(to_y, "y", 0, 0)

    stays, leaves = call(
        back_kernel,
        [((half, width), f32)] * 2,
        flag, first, second, gate_eff, up_eff,
        scalars=1,
    )
    got = lax.ppermute(leaves, "core", swap)
    (back,) = call(core_sum_kernel, [((nx, half // nx + EXTRA, width), i16)], stays, got)
    back, first, second, own, other = lax.optimization_barrier(
        (back, first, second, own, other)
    )
    back = lax.all_to_all(back, "x", 0, 0)
    (back,) = call(x_sum_kernel, [((nzlo, rows, width), f32)], back)
    back = lax.all_to_all(back, "zlo", 0, 0)
    (back,) = call(last_sum_kernel, [((rows, width), bf16)], back)

    def units(block):
        block = block.reshape(ny, 3, quarter, half)
        return block.transpose(1, 0, 2, 3).reshape(3, hidden_units, half)

    first, second = units(first), units(second)
    kept_side = jnp.where(own_kept, own, other)
    sent_side = jnp.where(own_kept, other, own)

    def weight_grad(member, side):
        return dot(first[member], kept_side[side], ((1,), (0,))) + dot(
            second[member], sent_side[side], ((1,), (0,))
        )

    grad_gate = jnp.where(gate_mask > 0.5, weight_grad(1, 0), 0.0).astype(bf16)
    grad_up = jnp.where(up_mask > 0.5, weight_grad(2, 0), 0.0).astype(bf16)
    grad_down = jnp.where(down_mask > 0.5, weight_grad(0, 1), 0.0).astype(bf16)
    return (back, grad_gate.T, grad_up.T, grad_down)


def solution(mesh):
    fine = Mesh(
        np.asarray(mesh.devices).reshape(4, 4, 8, 4, 2), ("zhi", "y", "zlo", "x", "core")
    )
    row, col = ("zhi", "y"), ("zlo", "x", "core")
    return jax.shard_map(
        body,
        mesh=fine,
        in_specs=(
            P(col, row),
            P(col, row),
            P(row, col),
            P(row, col),
            P(col, row),
            P(row, col),
            P(row, col),
            P(col, row),
        ),
        out_specs=(P(col, row), P(row, col), P(row, col), P(col, row)),
        check_vma=False,
    )
```

```python
import jax
import jax.numpy as jnp
import numpy as np
from jax import lax
from jax.experimental import pallas as pl
from jax.experimental.pallas import tpu as pltpu
from jax.sharding import Mesh, PartitionSpec as P

bf16 = jnp.bfloat16
f32 = jnp.float32
keep_sets = ((0, 1, 2), (0, 3, 4), (1, 3, 5), (2, 4, 5))


def keep_planes(pattern, axis):
    planes = []
    for members in keep_sets:
        kept = pattern == members[0]
        for member in members[1:]:
            kept = kept | (pattern == member)
        planes.append(jnp.where(kept, 1.0, 0.0).astype(bf16))
    return jnp.concatenate(planes, axis=axis)


def spread_matrix(size, axis):
    place = lax.broadcasted_iota(jnp.int32, (size, size), axis)
    source = lax.broadcasted_iota(jnp.int32, (size, size), 1 - axis)
    moved = (place >> 2) + (place & 3) * (size // 4) == source
    return jnp.where(moved, 1.0, 0.0).astype(bf16)


def dot(a, b, dims):
    return lax.dot_general(a, b, (dims, ((), ())), preferred_element_type=f32)


def zhi_exchange(block, flip0, flip1):
    pairs = [
        (z * 2 + c, (z ^ (flip0, flip1)[c]) * 2 + c) for z in range(4) for c in range(2)
    ]
    return lax.ppermute(block, ("zhi", "core"), pairs)


EXTRA = 16
COST = 2 * 10**10


def pack(values):
    rows, powers = [], []
    for value in values:
        most = jnp.max(jnp.abs(value), axis=0, keepdims=True)
        power = jnp.ceil(jnp.log2(jnp.maximum(most, 1e-30))) - 14.0
        rows.append(to_int16(jnp.round(value * jnp.exp2(-power))))
        powers.append(power)
    spot = lax.broadcasted_iota(jnp.int32, (EXTRA, values[0].shape[1]), 0)
    tail = jnp.where(spot == 0, powers[0], jnp.where(spot == 1, powers[1], powers[2]))
    return rows, to_int16(tail)


def to_int16(values):
    return values.astype(jnp.int32).astype(jnp.int16)


def wide(block):
    return block.astype(jnp.int32).astype(f32)


def unpack(block, units):
    powers = wide(block[3 * units : 3 * units + EXTRA, :])
    return [
        wide(block[i * units : (i + 1) * units, :]) * jnp.exp2(powers[i : i + 1, :])
        for i in range(3)
    ]


def mask_kernel(*refs):
    patterns, weights, kept, masks = refs[:3], refs[3:6], refs[6:9], refs[9:]
    units, width = weights[0].shape
    across, down = spread_matrix(width, 1), spread_matrix(units, 0)
    for i in range(3):
        if i < 2:
            mask = dot(keep_planes(patterns[i][...], 1), across, ((1,), (0,)))
        else:
            mask = dot(down, keep_planes(patterns[i][...], 0), ((1,), (0,)))
        masks[i][...] = mask.astype(bf16)
        kept[i][...] = jnp.where(mask > 0.5, weights[i][...].astype(f32), 0.0).astype(bf16)


def spread_kernel(block_ref, out_ref):
    for c in range(out_ref.shape[0]):
        out_ref[c] = block_ref[...]


def partial_kernel(flag_ref, gate_ref, up_ref, down_ref, own_ref, other_ref, out_ref):
    ny, units = out_ref.shape[0], gate_ref.shape[0] // out_ref.shape[0]
    is_own = flag_ref[0] == 1
    tokens = jnp.where(is_own, own_ref[0], other_ref[0])
    grad_out = jnp.where(is_own, own_ref[1], other_ref[1])
    products = [
        dot(gate_ref[...], tokens, ((1,), (1,))),
        dot(up_ref[...], tokens, ((1,), (1,))),
        dot(down_ref[...], grad_out, ((1,), (1,))),
    ]
    for c in range(ny):
        store([p[c * units : (c + 1) * units] for p in products], out_ref.at[c])


def store(values, send_ref):
    units = values[0].shape[0]
    rows, tail = pack(values)
    for i in range(3):
        send_ref[i * units : (i + 1) * units, :] = rows[i]
    send_ref[3 * units :, :] = tail


def sum_over_blocks(block_ref):
    units = (block_ref.shape[1] - EXTRA) // 3
    total = [0.0, 0.0, 0.0]
    for c in range(block_ref.shape[0]):
        parts = unpack(block_ref.at[c], units)
        total = [total[i] + parts[i] for i in range(3)]
    return total


def sent_sum_kernel(block_ref, send_ref):
    store(sum_over_blocks(block_ref), send_ref)


def kept_sum_kernel(block_ref, got_ref, total_ref, send_ref):
    total = sum_over_blocks(block_ref)
    parts = unpack(got_ref, total_ref.shape[1])
    total = [total[i] + parts[i] for i in range(3)]
    for i in range(3):
        total_ref[i] = total[i]
    store(total, send_ref)


def swiglu_kernel(total_ref, got_ref, out_ref, spread_ref):
    units = total_ref.shape[1]
    parts = unpack(got_ref, units)
    gate_pre, up_pre, hidden_grad = [total_ref[i] + parts[i] for i in range(3)]
    sigmoid_gate = jax.nn.sigmoid(gate_pre)
    silu_gate = gate_pre * sigmoid_gate
    results = (
        silu_gate * up_pre,
        hidden_grad * up_pre * sigmoid_gate * (1.0 + gate_pre * (1.0 - sigmoid_gate)),
        hidden_grad * silu_gate,
    )
    for i, result in enumerate(results):
        result = result.astype(bf16)
        out_ref[i * units : (i + 1) * units, :] = result
        for c in range(spread_ref.shape[0]):
            spread_ref[c, i * units : (i + 1) * units, :] = result


def back_product(block_ref, gate_ref, up_ref):
    ny, units = block_ref.shape[0], block_ref.shape[1] // 3

    def member(i):
        return jnp.concatenate(
            [block_ref[c, i * units : (i + 1) * units, :] for c in range(ny)], axis=0
        )

    return dot(member(1), gate_ref[...], ((0,), (0,))) + dot(
        member(2), up_ref[...], ((0,), (0,))
    )


def back_kernel(flag_ref, first_ref, second_ref, gate_ref, up_ref, stays_ref, leaves_ref):
    first = back_product(first_ref, gate_ref, up_ref)
    second = back_product(second_ref, gate_ref, up_ref)
    first_stays = flag_ref[0] == 1
    stays_ref[...] = jnp.where(first_stays, first, second)
    leaves_ref[...] = jnp.where(first_stays, second, first)


def core_sum_kernel(stays_ref, got_ref, send_ref):
    rows = send_ref.shape[1] - EXTRA
    for c in range(send_ref.shape[0]):
        part = slice(c * rows, (c + 1) * rows)
        value = stays_ref[part, :] + got_ref[part, :]
        most = jnp.max(jnp.abs(value), axis=0, keepdims=True)
        power = jnp.ceil(jnp.log2(jnp.maximum(most, 1e-30))) - 14.0
        send_ref[c, :rows, :] = to_int16(jnp.round(value * jnp.exp2(-power)))
        send_ref[c, rows:, :] = to_int16(jnp.broadcast_to(power, (EXTRA, value.shape[1])))


def x_sum_kernel(block_ref, out_ref):
    rows = block_ref.shape[1] - EXTRA
    total = 0.0
    for c in range(block_ref.shape[0]):
        powers = wide(block_ref[c, rows:, :])
        total = total + wide(block_ref[c, :rows, :]) * jnp.exp2(powers[:1, :])
    count, each = out_ref.shape[0], out_ref.shape[1]
    for c in range(count):
        out_ref[c] = total[c * each : (c + 1) * each]


def last_sum_kernel(block_ref, out_ref):
    total = block_ref[0]
    for c in range(1, block_ref.shape[0]):
        total = total + block_ref[c]
    out_ref[...] = total.astype(bf16)


def call(kernel, outs, *args, scalars=0):
    specs = [pl.BlockSpec(memory_space=pltpu.SMEM)] * scalars
    specs += [pl.BlockSpec()] * (len(args) - scalars)
    return pl.pallas_call(
        kernel,
        in_specs=specs,
        out_shape=[jax.ShapeDtypeStruct(shape, kind) for shape, kind in outs],
        compiler_params=pltpu.CompilerParams(vmem_limit_bytes=32 * 2**20),
        cost_estimate=pl.CostEstimate(flops=COST, bytes_accessed=1024, transcendentals=0),
    )(*args)


def body(inputs, cotangent, gate_weight, up_weight, down_weight, gate_pattern, up_pattern, down_pattern):
    sizes = {"zhi": 4, "y": 4, "zlo": 8, "x": 4, "core": 2}
    rows, width = inputs.shape
    hidden_units = down_weight.shape[0]
    half = rows * sizes["zlo"] * sizes["x"]
    ny = sizes["y"]
    quarter = hidden_units // ny
    swap = [(0, 1), (1, 0)]
    nx, nzlo = sizes["x"], sizes["zlo"]
    both = jnp.stack([inputs, cotangent])
    both = jnp.broadcast_to(both[None], (nzlo, *both.shape))
    both = lax.all_to_all(both, "zlo", 0, 0)
    both, gate_pattern, up_pattern, down_pattern = lax.optimization_barrier(
        (both, gate_pattern, up_pattern, down_pattern)
    )
    (both,) = call(spread_kernel, [((nx, nzlo, 2, rows, width), bf16)], both)
    both = lax.all_to_all(both, "x", 0, 0)

    gate_eff, up_eff, down_eff, gate_mask, up_mask, down_mask = call(
        mask_kernel,
        [((hidden_units, width), bf16)] * 6,
        gate_pattern.T, up_pattern.T, down_pattern,
        gate_weight.T, up_weight.T, down_weight,
    )

    both, gate_eff, up_eff, down_eff = lax.optimization_barrier(
        (both, gate_eff, up_eff, down_eff)
    )
    own = both.transpose(2, 0, 1, 3, 4).reshape(2, half, width)
    other = lax.ppermute(own, "core", swap)

    zhi, core = lax.axis_index("zhi"), lax.axis_index("core")
    keep = jnp.where(core == 0, (zhi ^ (zhi >> 1)) & 1, zhi >> 1)
    own_kept = keep == core
    flag = own_kept.astype(jnp.int32).reshape(1)

    i16 = jnp.int16
    packed = 3 * quarter + EXTRA
    block = [((ny, packed, half), i16)]
    operands = (gate_eff, up_eff, down_eff, own, other)
    (sent,) = call(partial_kernel, block, 1 - flag, *operands, scalars=1)
    (kept,) = call(partial_kernel, block, flag, *operands, scalars=1)
    sent = lax.all_to_all(sent, "y", 0, 0)
    (send,) = call(sent_sum_kernel, [((packed, half), i16)], sent)
    kept, send = lax.optimization_barrier((kept, send))
    got = zhi_exchange(send, 1, 3)
    kept = lax.all_to_all(kept, "y", 0, 0)
    total, send = call(
        kept_sum_kernel, [((3, quarter, half), f32), ((packed, half), i16)], kept, got
    )
    got = zhi_exchange(send, 3, 1)
    spread = ((ny, 3 * quarter, half), bf16)
    mine, to_y = call(swiglu_kernel, [((3 * quarter, half), bf16), spread], total, got)
    theirs = zhi_exchange(mine, 1, 3)
    first = lax.all_to_all(to_y, "y", 0, 0)
    (to_y,) = call(spread_kernel, [spread], theirs)
    second = lax.all_to_all(to_y, "y", 0, 0)

    stays, leaves = call(
        back_kernel,
        [((half, width), f32)] * 2,
        flag, first, second, gate_eff, up_eff,
        scalars=1,
    )
    got = lax.ppermute(leaves, "core", swap)
    (back,) = call(core_sum_kernel, [((nx, half // nx + EXTRA, width), i16)], stays, got)
    back, first, second = lax.optimization_barrier((back, first, second))
    back = lax.all_to_all(back, "x", 0, 0)
    (back,) = call(x_sum_kernel, [((nzlo, rows, width), f32)], back)
    back = lax.all_to_all(back, "zlo", 0, 0)
    (back,) = call(last_sum_kernel, [((rows, width), bf16)], back)

    def units(block):
        block = block.reshape(ny, 3, quarter, half)
        return block.transpose(1, 0, 2, 3).reshape(3, hidden_units, half)

    first, second = units(first), units(second)
    kept_side = jnp.where(own_kept, own, other)
    sent_side = jnp.where(own_kept, other, own)

    def weight_grad(member, side):
        return dot(first[member], kept_side[side], ((1,), (0,))) + dot(
            second[member], sent_side[side], ((1,), (0,))
        )

    grad_gate = jnp.where(gate_mask > 0.5, weight_grad(1, 0), 0.0).astype(bf16)
    grad_up = jnp.where(up_mask > 0.5, weight_grad(2, 0), 0.0).astype(bf16)
    grad_down = jnp.where(down_mask > 0.5, weight_grad(0, 1), 0.0).astype(bf16)
    return (back, grad_gate.T, grad_up.T, grad_down)


def solution(mesh):
    fine = Mesh(
        np.asarray(mesh.devices).reshape(4, 4, 8, 4, 2), ("zhi", "y", "zlo", "x", "core")
    )
    row, col = ("zhi", "y"), ("zlo", "x", "core")
    return jax.shard_map(
        body,
        mesh=fine,
        in_specs=(
            P(col, row),
            P(col, row),
            P(row, col),
            P(row, col),
            P(col, row),
            P(row, col),
            P(row, col),
            P(col, row),
        ),
        out_specs=(P(col, row), P(row, col), P(row, col), P(col, row)),
        check_vma=False,
    )
```
